32 devices in a mesh: rep: 2 (over y), ep: 4 (over z), node: 2 (over x), sub: 2 (over core).
Axes of the slice: x: 2, y: 2, z: 4, core: 2. Of those that a mesh axis runs over, the one named last changes fastest.
Arguments:
- tokens: bfloat16 [1024, 7168], P(('rep', 'ep', 'node'), 'sub'), parts along dimension 0, may hold values from -6 to 6
- routes: int32 [1024, 2], P(('rep', 'ep', 'node')), parts along dimension 0, may hold values from 0 to 3, all different within a row; in each aligned block of 64 rows (0 to 63, 64 to 127, ...) at most 40 rows name the same one
- tenant: int32 [1024], P(('rep', 'ep', 'node')), parts along dimension 0, may hold values from 0 to 7
- expert_place: int32 [4], replicated, may hold values from 0 to 3, each once
- router_weight: bfloat16 [7168, 4], P('sub'), may hold values from -0.0625 to 0.0625
- adapter_down: bfloat16 [7168, 128], P('sub'), may hold values from -0.0625 to 0.0625
- adapter_up: bfloat16 [128, 4], replicated, may hold values from -1.5 to 1.5
- gate_weight: bfloat16 [4, 7168, 1024], P('ep', 'sub', 'node'), may hold values from -0.0625 to 0.0625
- up_weight: bfloat16 [4, 7168, 1024], P('ep', 'sub', 'node'), may hold values from -0.0625 to 0.0625
- down_weight: bfloat16 [4, 2, 1024, 3584], P('ep', 'sub', None, 'node'), may hold values from -0.1875 to 0.1875
Outputs:
- mixed: bfloat16 [1024, 7168], P(('rep', 'ep', 'node'), 'sub'), parts along dimension 0
The draws below stay inside these ranges and needn't reach their ends.
There are 2 independent parts, one for each index of `rep`. The reference program is written for one: setup_inputs(seed, part) draws one part's arguments, and reference() takes and returns one part's arrays. A program takes and returns all parts, laid end to end along the dimension named above; an argument that names none is the same for every part. Nothing has to cross between parts.
Inputs may be any that keep to these rules, and one draw needn't show every extreme that they name: `routes`: each row names 2 different experts. Within the rows of one device (aligned blocks of 64 rows) no expert is named by more than 40 rows, a bound that some block reaches. `expert_place`: A permutation: each index of ep holds exactly one expert.
All inputs are finite; a program needn't handle non-finite values.
Results may differ from the reference program's by a relative error of at most 0.0057.
Values may be sent and summed in bfloat16 or wider, within the bound.
No kernel may reach another device: no remote copies, remote signals or barrier semaphores. Data moves between devices by JAX's collectives and lax.ppermute only.
A program may use at most 128 MiB of HBM per device.

```python
import math
import jax
import jax.numpy as jnp
import numpy as np
from jax import lax

D = 7168
FF = 1024
TOPK = 2
RANK = 16
TENANTS = 8
TOK_DEV = 64
EXPERTS = 4
TOKENS = 512
CAP = 40
N_EP = 4
N_NODE = 2
N_SUB = 2


def place_ends(values, rng, low, top_value):
    extent = values.shape
    place = [jax.random.randint(jax.random.fold_in(rng, axis), (), 0, extent[axis]) for axis in range(len(extent))]
    values = values.at[tuple(place)].set(low)
    longest = extent.index(max(extent))
    place[longest] = (place[longest] + 1) % extent[longest]
    return values.at[tuple(place)].set(top_value)


def block_scale(rng, shape, pieces, least, largest):
    loudness = 1.0
    for dim, parts in pieces:
        steps = jax.random.uniform(jax.random.fold_in(jax.random.fold_in(rng, 6), dim), (parts,), jnp.float32, least / len(pieces), largest / len(pieces))
        loudness = loudness * jnp.repeat(jnp.exp(steps), shape[dim] // parts).reshape((-1,) + (1,) * (len(shape) - 1 - dim))
    return loudness


def deal_out(rng, own, number, rows, amount, top, reach, skew):
    sequence = jax.random.permutation(rng, amount)
    crowded, common = shares(amount, rows * top, reach, skew, True), shares(amount, rows * top, reach, skew, False)
    places = jnp.arange(amount)

    def named(tallies, turn):
        used = int((tallies > 0).sum())
        fixed = max(1, used // 4)
        moved = fixed + (places - fixed + turn * (used - fixed)) % max(1, amount - fixed)
        return jnp.zeros((amount,), jnp.int32).at[sequence[jnp.where(places < fixed, places, moved)]].set(jnp.asarray(tallies, jnp.int32))

    tallies = jnp.where(number % 4 == 0, named(crowded, number // 4), named(common, number - number // 4 - 1))
    mixed = jax.random.permutation(jax.random.fold_in(own, 3), amount)
    source_of, sink = mixed[0:amount // 2 * 2:2], mixed[1:amount // 2 * 2:2]
    margin = jnp.minimum(tallies[source_of] - 1, reach - tallies[sink]) // 2
    margin = jnp.where((source_of == sequence[0]) | (sink == sequence[0]) | (tallies[sink] == 0), 0, jnp.maximum(margin, 0))
    moved = jax.random.randint(jax.random.fold_in(own, 4), (amount // 2,), 0, 1 << 20) % (margin + 1)
    tallies = tallies.at[source_of].add(-moved).at[sink].add(moved)
    items = jnp.searchsorted(jnp.cumsum(tallies), jnp.arange(rows * top), side="right").astype(jnp.int32)
    grid = items.reshape(top, rows).T
    grid = grid[jax.random.permutation(jax.random.fold_in(own, 1), rows)]
    turn = jax.random.randint(jax.random.fold_in(own, 2), (rows, 1), 0, top)
    return jnp.take_along_axis(grid, (jnp.arange(top)[None, :] + turn) % top, axis=1)


def shares(amount, total, limit, slope, full):
    portions = [(1 << 20) // math.isqrt(standing ** slope) + 1 for standing in range(1, amount + 1)]
    largest = limit if full else min(limit, max(-(-total // amount), total * portions[0] // sum(portions)))
    least = 1 if total - largest >= amount - 1 else 0
    given, rest = [largest] + [least] * (amount - 1), total - largest - least * (amount - 1)
    while rest > 0:
        free = [i for i in range(1, amount) if given[i] < largest] or [i for i in range(1, amount) if given[i] < limit]
        whole, remaining = sum([portions[i] for i in free]), rest
        for i in free:
            extra = min(limit - given[i], max(1, remaining * portions[i] // whole), rest)
            given[i] = given[i] + extra
            rest = rest - extra
    return np.array(given)


def normal_values(key, shape, scale, reach, shards=(), kind=jnp.bfloat16):
    result = jax.random.normal(key, shape, jnp.float32) * scale
    if len(shards) > 0:
        result = block_scale(key, shape, shards, -0.22, 0.18) * result
    return jnp.clip(result, min=-reach, max=reach).astype(kind)


def setup_inputs(seed: int = 0, part: int = 0) -> dict:
    arg_keys = jax.random.split(jax.random.key(seed), 11)
    part_splits = jax.random.split(jax.random.fold_in(arg_keys[10], part), 11)
    tokens = normal_values(part_splits[0], (TOKENS, D), 1.0, 6.0, ((0, 8), (1, 2)))
    routes_keys = jax.random.split(jax.random.fold_in(part_splits[1], 1), TOKENS // TOK_DEV)
    routes_turns = jax.random.permutation(jax.random.fold_in(part_splits[1], 3), TOKENS // TOK_DEV)
    routes = jax.vmap(lambda own, number: deal_out(jax.random.fold_in(part_splits[1], 2), own, number, TOK_DEV, EXPERTS, TOPK, CAP, 2))(routes_keys, routes_turns).reshape((TOKENS, TOPK))
    tenant = place_ends(jax.random.randint(part_splits[2], (TOKENS,), 0, TENANTS), jax.random.fold_in(part_splits[2], 1), 0, TENANTS - 1).astype(jnp.int32)
    expert_place = jax.random.permutation(arg_keys[3], EXPERTS).astype(jnp.int32)
    router_weight = normal_values(arg_keys[4], (D, EXPERTS), D ** -0.5, 0.0625, ((0, 2),))
    adapter_down = normal_values(arg_keys[5], (D, TENANTS * RANK), D ** -0.5, 0.0625, ((0, 2),))
    adapter_up = normal_values(arg_keys[6], (TENANTS * RANK, EXPERTS), RANK ** -0.5, 1.5)
    gate_weight = normal_values(arg_keys[7], (EXPERTS, D, FF), D ** -0.5, 0.0625, ((0, 4), (1, 2), (2, 2)))
    up_weight = normal_values(arg_keys[8], (EXPERTS, D, FF), D ** -0.5, 0.0625, ((0, 4), (1, 2), (2, 2)))
    down_weight = normal_values(arg_keys[9], (EXPERTS, N_SUB, FF, D // N_SUB), FF ** -0.5, 0.1875, ((0, 4), (1, 2), (3, 2)))
    return {"tokens": tokens, "routes": routes, "tenant": tenant, "expert_place": expert_place, "router_weight": router_weight, "adapter_down": adapter_down, "adapter_up": adapter_up, "gate_weight": gate_weight, "up_weight": up_weight, "down_weight": down_weight}


route_scale = 2.5


def reference(tokens, routes, tenant, expert_place, router_weight, adapter_down, adapter_up, gate_weight, up_weight, down_weight):
    base = jnp.dot(tokens, router_weight, preferred_element_type=jnp.float32)
    lowrank = jnp.dot(tokens, adapter_down, preferred_element_type=jnp.float32)
    column_owner = jnp.arange(TENANTS * RANK, dtype=jnp.int32) // RANK
    lowrank = jnp.where(column_owner[None, :] == tenant[:, None], lowrank, jnp.float32(0.0))
    logits = base + jnp.dot(lowrank, adapter_up.astype(jnp.float32), precision=lax.Precision.HIGHEST)
    picked = jnp.take_along_axis(logits, routes, axis=1)
    score = jax.nn.sigmoid(picked)
    weight = route_scale * score / jnp.sum(score, axis=1, keepdims=True)
    flat = routes.reshape(-1).astype(jnp.int32)
    blocks = TOKENS // TOK_DEV
    onehot = (flat[:, None] == jnp.arange(EXPERTS, dtype=jnp.int32)[None, :]).astype(jnp.int32)
    counts = jnp.cumsum(onehot.reshape(blocks, TOK_DEV * TOPK, EXPERTS), axis=1).reshape(-1, EXPERTS)
    rank = jnp.sum((counts - 1) * onehot, axis=1).astype(jnp.int32)
    slot = expert_place.astype(jnp.int32)[flat]
    block_of = jnp.arange(TOKENS * TOPK, dtype=jnp.int32) // (TOK_DEV * TOPK)
    per_expert = N_EP * N_NODE * CAP
    position = (slot * per_expert + block_of * CAP + rank).astype(jnp.int32)
    token_of = jnp.arange(TOKENS * TOPK, dtype=jnp.int32) // TOPK
    table = jnp.zeros((EXPERTS * per_expert, D), jnp.bfloat16).at[position].set(tokens[token_of])
    table = table.reshape(EXPERTS, per_expert, D)

    def expert(operands):
        rows, w_gate, w_up, w_down = operands
        gate = jnp.dot(rows, w_gate, preferred_element_type=jnp.float32)
        up = jnp.dot(rows, w_up, preferred_element_type=jnp.float32)
        hidden = (jax.nn.silu(gate) * up).astype(jnp.bfloat16)
        full_down = jnp.transpose(w_down, (1, 0, 2)).reshape(FF, D)
        return jnp.dot(hidden, full_down, preferred_element_type=jnp.float32).astype(jnp.bfloat16)

    outputs = lax.map(expert, (table, gate_weight, up_weight, down_weight))
    chosen = outputs.reshape(-1, D)[position].astype(jnp.float32).reshape(TOKENS, TOPK, D)
    mixed = jnp.sum(chosen * weight[:, :, None], axis=1)
    return mixed.astype(jnp.bfloat16)
```

```python
import jax
import jax.numpy as jnp
from jax import lax
from jax.sharding import PartitionSpec as P

RANK = 16
ROUTE_SCALE = 2.5
f32 = jnp.float32
bf16 = jnp.bfloat16


def partner(index, step):
    return index ^ step


def swap(value, axis, step):
    count = lax.axis_size(axis)
    return lax.ppermute(value, axis, [(i, partner(i, step)) for i in range(count)])


def in_index_order(parts, index):
    parts = list(parts)
    bit = 1
    while bit < len(parts):
        flip = (index & bit) != 0
        parts = [jnp.where(flip, parts[j ^ bit], parts[j]) for j in range(len(parts))]
        bit *= 2
    return parts


def after(value, *others):
    return lax.optimization_barrier((value,) + others)[0]


def body(
    tokens,
    routes,
    tenant,
    expert_place,
    router_weight,
    adapter_down,
    adapter_up,
    gate_weight,
    up_weight,
    down_weight,
):
    tok_rows, half_width = tokens.shape
    topk = routes.shape[1]
    experts = router_weight.shape[1]
    eps = lax.axis_size("ep")
    nodes = lax.axis_size("node")
    cap = 5 * tok_rows * topk // (4 * eps)
    hidden_dev = gate_weight.shape[2]
    out_width = down_weight.shape[3]
    ep_me = lax.axis_index("ep")
    node_me = lax.axis_index("node")

    expert_of_block = jnp.argmax(
        expert_place[None, :] == (jnp.arange(eps, dtype=jnp.int32) ^ ep_me)[:, None], axis=1
    ).astype(jnp.int32)
    routes_t = routes.T
    named = jnp.any(routes_t[None] == expert_of_block[:, None, None], axis=1)
    earlier = (
        lax.broadcasted_iota(jnp.int32, (tok_rows, tok_rows), 0)
        < lax.broadcasted_iota(jnp.int32, (tok_rows, tok_rows), 1)
    ).astype(bf16)
    before = jnp.dot(named.astype(bf16), earlier, preferred_element_type=f32)
    place = jnp.where(named, before, f32(-1.0))
    row = lax.broadcasted_iota(jnp.int32, (1, cap, 1), 1).astype(f32)
    placing = (place[:, None, :] == row).astype(bf16).reshape(eps * cap, tok_rows)
    outgoing = jnp.dot(placing, tokens, preferred_element_type=f32).astype(bf16)
    outgoing = outgoing.reshape(eps, cap, half_width)

    order = list(range(eps))
    mine = [outgoing[0]] + [None] * (eps - 1)
    for k in order[1:]:
        mine[k] = swap(outgoing[k], "ep", k)
    blocks = []
    for k in order:
        blocks.append([mine[k]] + [swap(mine[k], "node", j) for j in range(1, nodes)])

    gate_w, up_w, down_w = gate_weight[0], up_weight[0], down_weight[0, 0]
    chunks = CHUNKS(eps)
    returned = [None] * eps
    for chunk in chunks:
        rows = jnp.concatenate([blocks[k][j] for j in range(nodes) for k in chunk], axis=0)
        gate = jnp.dot(rows, gate_w, preferred_element_type=f32)
        up = jnp.dot(rows, up_w, preferred_element_type=f32)
        theirs = swap(jnp.concatenate([gate.astype(bf16), up.astype(bf16)], axis=1), "sub", 1)
        gate = gate + theirs[:, :hidden_dev].astype(f32)
        up = up + theirs[:, hidden_dev:].astype(f32)
        hidden = (jax.nn.silu(gate) * up).astype(bf16)
        groups = hidden.reshape(nodes, len(chunk) * cap, hidden_dev)
        by_node = [hidden]
        for i in range(1, nodes):
            got = swap(groups, "node", i)
            by_node.append(jnp.concatenate([got[j ^ i] for j in range(nodes)], axis=0))
        full = jnp.concatenate(in_index_order(by_node, node_me), axis=1)
        out = jnp.dot(full, down_w, preferred_element_type=f32).astype(bf16)
        out = out.reshape(nodes, len(chunk), cap, out_width)
        for i, k in enumerate(chunk):
            part = out[:, i]
            returned[k] = part if k == 0 else swap(part, "ep", k)

    base = jnp.dot(tokens, router_weight, preferred_element_type=f32)
    lowrank = jnp.dot(tokens, adapter_down, preferred_element_type=f32)
    column_owner = lax.broadcasted_iota(jnp.int32, (1, adapter_down.shape[1]), 1) // RANK
    lowrank = jnp.where(column_owner == tenant[:, None], lowrank, f32(0.0))
    logits = base + jnp.dot(lowrank, adapter_up.astype(f32), precision=lax.Precision.HIGHEST)
    logits = logits + swap(logits, "sub", 1)
    score = jax.nn.sigmoid(logits).T
    chosen = jnp.any(
        routes_t[None] == lax.broadcasted_iota(jnp.int32, (experts, 1, 1), 0), axis=1
    )
    score = jnp.where(chosen, score, f32(0.0))
    weight = ROUTE_SCALE * score / jnp.sum(score, axis=0, keepdims=True)
    to_block = expert_of_block[:, None] == jnp.arange(experts, dtype=jnp.int32)[None, :]
    weight = jnp.sum(jnp.where(to_block[:, :, None], weight[None], f32(0.0)), axis=1)
    info = jnp.stack([place, weight])
    infos = [info] + [swap(info, "node", j) for j in range(1, nodes)]

    back = jnp.stack(returned, axis=1).reshape(nodes, eps * cap, out_width)
    mixed = []
    for j in range(nodes):
        hit = infos[j][0][:, None, :] == row
        weighted = jnp.where(hit, infos[j][1][:, None, :], f32(0.0)).reshape(eps * cap, tok_rows)
        high = weighted.astype(bf16)
        low = (weighted - high.astype(f32)).astype(bf16)
        dims = (((0,), (0,)), ((), ()))
        total = lax.dot_general(high, back[j], dims, preferred_element_type=f32)
        total = total + lax.dot_general(low, back[j], dims, preferred_element_type=f32)
        part = total.astype(bf16)
        mixed.append(part if j == 0 else swap(part, "node", j))
    return jnp.concatenate(in_index_order(mixed, node_me), axis=1)


def CHUNKS(eps):
    return [list(range(eps))]


def solution(mesh):
    placed = (
        P(("rep", "ep", "node"), "sub"),
        P(("rep", "ep", "node"), None),
        P(("rep", "ep", "node")),
        P(),
        P("sub", None),
        P("sub", None),
        P(),
        P("ep", "sub", "node"),
        P("ep", "sub", "node"),
        P("ep", "sub", None, "node"),
    )
    return jax.shard_map(
        body, mesh=mesh, in_specs=placed, out_specs=P(("rep", "ep", "node"), "sub"), check_vma=False
    )
```

```python
import functools

import jax
import jax.numpy as jnp
from jax import lax
from jax.experimental import pallas as pl
from jax.experimental.pallas import tpu as pltpu
from jax.sharding import PartitionSpec as P

RANK = 16
ROUTE_SCALE = 2.5
VMEM_LIMIT = 24 * 1024 * 1024
f32 = jnp.float32
bf16 = jnp.bfloat16


def partner(index, step):
    return index ^ step


def swap(value, axis, step):
    count = lax.axis_size(axis)
    return lax.ppermute(value, axis, [(i, partner(i, step)) for i in range(count)])


def send(value, ep_step, node_step):
    if not ep_step and not node_step:
        return value
    if not node_step:
        return swap(value, "ep", ep_step)
    if not ep_step:
        return swap(value, "node", node_step)
    eps, nodes = lax.axis_size("ep"), lax.axis_size("node")
    pairs = [
        (i * nodes + j, partner(i, ep_step) * nodes + partner(j, node_step))
        for i in range(eps)
        for j in range(nodes)
    ]
    return lax.ppermute(value, ("ep", "node"), pairs)


def regroup(rows, step, size):
    count = rows.shape[0] // size
    return jnp.concatenate([rows[(j ^ step) * size : (j ^ step) * size + size] for j in range(count)])


WHOLE = pl.BlockSpec(memory_space=pltpu.VMEM)
ANY = pl.BlockSpec(memory_space=pl.ANY)
IN_HBM = pl.BlockSpec(memory_space=pltpu.HBM)


def call(kernel, out_shape, in_specs, scratch=(), aliases=None):
    return pl.pallas_call(
        kernel,
        out_shape=out_shape,
        in_specs=in_specs,
        out_specs=[ANY if i in (aliases or {}).values() else WHOLE for i in range(len(out_shape))],
        scratch_shapes=list(scratch),
        input_output_aliases=aliases or {},
        compiler_params=pltpu.CompilerParams(vmem_limit_bytes=VMEM_LIMIT),
        cost_estimate=pl.CostEstimate(flops=0, bytes_accessed=0, transcendentals=0),
    )


def in_hbm(value):
    return pltpu.with_memory_space_constraint(value, pltpu.HBM)


def pack_rows(expert_place, routes_t, tokens, order, cap, behind=()):
    experts = expert_place.shape[0]
    topk, tok_rows = routes_t.shape
    width = tokens.shape[1]

    def kernel(where_hbm, routes_hbm, tokens_hbm, *refs):
        place_ref, *refs = refs[len(behind) :]
        block_refs, (where_ref, routes_ref, tokens_ref, sems) = refs[: len(order)], refs[len(order) :]
        pairs = [(where_hbm, where_ref), (routes_hbm, routes_ref), (tokens_hbm, tokens_ref)]
        copies = [pltpu.make_async_copy(a, b, sems.at[i]) for i, (a, b) in enumerate(pairs)]
        for copy in copies:
            copy.start()
        copies[0].wait()
        copies[1].wait()
        named_by = routes_ref[...]
        where = where_ref[...] ^ lax.axis_index("ep")
        relative = jnp.zeros_like(named_by)
        for e in range(experts):
            relative = jnp.where(named_by == e, where[:, e : e + 1], relative)
        block = lax.broadcasted_iota(jnp.int32, (experts, tok_rows), 0)
        named = functools.reduce(
            jnp.logical_or, [relative[k : k + 1] == block for k in range(topk)]
        )
        earlier = lax.broadcasted_iota(jnp.int32, (tok_rows, tok_rows), 0) < (
            lax.broadcasted_iota(jnp.int32, (tok_rows, tok_rows), 1)
        )
        before = jnp.dot(
            jnp.where(named, f32(1.0), f32(0.0)).astype(bf16),
            jnp.where(earlier, f32(1.0), f32(0.0)).astype(bf16),
            preferred_element_type=f32,
        )
        place = jnp.where(named, before, f32(-1.0))
        place_ref[...] = place
        row = lax.broadcasted_iota(jnp.int32, (cap, tok_rows), 0).astype(f32)
        copies[2].wait()
        for block_ref, k in zip(block_refs, order):
            placing = jnp.where(place[k : k + 1] == row, f32(1.0), f32(0.0)).astype(bf16)
            block_ref[...] = jnp.dot(
                placing, tokens_ref[...], preferred_element_type=f32
            ).astype(bf16)

    shapes = [jax.ShapeDtypeStruct((experts, tok_rows), f32)]
    shapes += [jax.ShapeDtypeStruct((cap, width), bf16)] * len(order)
    scratch = [
        pltpu.VMEM((1, experts), jnp.int32),
        pltpu.VMEM((topk, tok_rows), jnp.int32),
        pltpu.VMEM((tok_rows, width), bf16),
        pltpu.SemaphoreType.DMA((3,)),
    ]
    return call(kernel, shapes, [IN_HBM] * 3 + [ANY] * len(behind), scratch)(
        in_hbm(expert_place.reshape(1, experts)), in_hbm(routes_t), in_hbm(tokens), *behind
    )


def hold(held, behind):
    count = len(behind)
    shapes = [jax.ShapeDtypeStruct(a.shape, a.dtype) for a in held]
    aliases = {count + i: i for i in range(len(held))}
    specs = [ANY] * (count + len(held))
    return call(lambda *refs: None, shapes, specs, aliases=aliases)(*behind, *held)


def load(arrays, behind):
    count = len(arrays)

    def kernel(*refs):
        fetch(refs[:count], refs[count + len(behind) : -1], refs[-1])

    shapes = [pltpu.VMEM(a.shape, a.dtype) for a in arrays]
    specs = [IN_HBM] * count + [ANY] * len(behind)
    return call(kernel, shapes, specs, [pltpu.SemaphoreType.DMA((count,))])(
        *[in_hbm(a) for a in arrays], *behind
    )


def as_column(row, size):
    same = lax.broadcasted_iota(jnp.int32, (size, size), 0) == (
        lax.broadcasted_iota(jnp.int32, (size, size), 1)
    )
    return jnp.sum(jnp.where(same, row, jnp.zeros_like(row)), axis=1, keepdims=True)


def fetch(sources, places, sems):
    copies = [pltpu.make_async_copy(a, b, sems.at[i]) for i, (a, b) in enumerate(zip(sources, places))]
    for copy in copies:
        copy.start()
    for copy in copies:
        copy.wait()


def partial_logits(tokens, tenant, router_weight, adapter_down, adapter_up, behind):
    tok_rows = tokens.shape[0]
    ranks, experts = adapter_up.shape
    given = [tokens, adapter_down, router_weight.T, adapter_up.T, tenant.reshape(1, tok_rows)]

    def kernel(*refs):
        out_ref, *held, sems = refs[len(given) + len(behind) :]
        fetch(refs[: len(given)], held, sems)
        tokens_ref, down_ref, router_ref, up_ref, tenant_ref = held
        lowrank = jnp.dot(tokens_ref[...], down_ref[...], preferred_element_type=f32)
        owner = (lax.broadcasted_iota(jnp.int32, (tok_rows, ranks), 1) // RANK).astype(f32)
        tenants = as_column(tenant_ref[...].astype(f32), tok_rows)
        lowrank = jnp.where(owner == tenants, lowrank, f32(0.0))
        across = (((1,), (1,)), ((), ()))
        base = lax.dot_general(
            router_ref[...], tokens_ref[...], across, preferred_element_type=f32
        )
        out_ref[...] = base + lax.dot_general(
            up_ref[...].astype(f32),
            lowrank,
            across,
            precision=lax.Precision.HIGHEST,
            preferred_element_type=f32,
        )

    shapes = [jax.ShapeDtypeStruct((experts, tok_rows), f32)]
    specs = [IN_HBM] * len(given) + [ANY] * len(behind)
    scratch = [pltpu.VMEM(a.shape, a.dtype) for a in given]
    scratch.append(pltpu.SemaphoreType.DMA((len(given),)))
    return call(kernel, shapes, specs, scratch)(*[in_hbm(a) for a in given], *behind)[0]


def route_info(parts, place, expert_place, routes_t):
    _, experts, tok_rows = parts.shape
    topk = routes_t.shape[0]
    given = [expert_place.reshape(1, experts), routes_t]

    def kernel(parts_ref, place_ref, where_hbm, routes_hbm, out_ref, where_ref, routes_ref, sems):
        fetch([where_hbm, routes_hbm], [where_ref, routes_ref], sems)
        score = jax.nn.sigmoid(functools.reduce(jnp.add, [parts_ref[i] for i in range(parts.shape[0])]))
        expert = lax.broadcasted_iota(jnp.int32, (experts, tok_rows), 0)
        chosen = functools.reduce(
            jnp.logical_or, [routes_ref[k : k + 1, :] == expert for k in range(topk)]
        )
        score = jnp.where(chosen, score, f32(0.0))
        weight = ROUTE_SCALE * score / jnp.sum(score, axis=0, keepdims=True)
        slot = where_ref[...] ^ lax.axis_index("ep")
        for r in range(experts):
            here = jnp.zeros((1, tok_rows), f32)
            for e in range(experts):
                here = jnp.where(slot[:, e : e + 1] == r, weight[e : e + 1], here)
            out_ref[0, :, r : r + 1] = as_column(place_ref[r : r + 1, :], tok_rows)
            out_ref[1, :, r : r + 1] = as_column(here, tok_rows)

    shapes = [jax.ShapeDtypeStruct((2, tok_rows, experts), f32)]
    scratch = [pltpu.VMEM(a.shape, a.dtype) for a in given]
    scratch.append(pltpu.SemaphoreType.DMA((len(given),)))
    return call(kernel, shapes, [WHOLE] * 2 + [IN_HBM] * 2, scratch)(
        parts, place, *[in_hbm(a) for a in given]
    )[0]


def activate(own, both):
    count, wide = own.shape

    def kernel(own_ref, both_ref, out_ref):
        total = own_ref[...] + both_ref[1 - lax.axis_index("sub")].astype(f32)
        gate, up = total[:, : wide // 2], total[:, wide // 2 :]
        out_ref[...] = (jax.nn.silu(gate) * up).astype(bf16)

    shapes = [jax.ShapeDtypeStruct((count, wide // 2), bf16)]
    return call(kernel, shapes, [WHOLE] * 2)(own, both)[0]


def dots(rows, weights, kinds, behind):
    count, wide = rows.shape[0], weights[0].shape[1]

    def kernel(rows_ref, *refs):
        for i in range(len(weights)):
            value = jnp.dot(rows_ref[...], refs[i][...], preferred_element_type=f32)
            for out in refs[len(weights) + len(behind) :]:
                out[:, i * wide : (i + 1) * wide] = value.astype(out.dtype)

    shapes = [jax.ShapeDtypeStruct((count, len(weights) * wide), kind) for kind in kinds]
    specs = [WHOLE] * (1 + len(weights)) + [ANY] * len(behind)
    return call(kernel, shapes, specs)(rows, *weights, *behind)


def project(by_node, weight, behind):
    nodes = len(by_node)
    count, part = by_node[0].shape

    def kernel(*refs):
        hidden_refs, weight_ref, out_ref = refs[:nodes], refs[nodes], refs[-1]
        node_me = lax.axis_index("node")
        total = None
        for i in range(nodes):
            node = node_me ^ i
            hidden = hidden_refs[i][...] if by_node[i].ndim == 2 else hidden_refs[i][node]
            at = pl.ds(pl.multiple_of(node * part, part), part)
            value = jnp.dot(hidden, weight_ref[at, :], preferred_element_type=f32)
            total = value if total is None else total + value
        out_ref[...] = total.astype(bf16)

    shapes = [jax.ShapeDtypeStruct((count, weight.shape[1]), bf16)]
    specs = [WHOLE] * (nodes + 1) + [ANY] * len(behind)
    return call(kernel, shapes, specs)(*by_node, weight, *behind)[0]


def weighted_sum(info, pieces):
    tok_rows = info.shape[1]
    total = None
    for k, value in pieces:
        row = lax.broadcasted_iota(jnp.int32, (tok_rows, value.shape[0]), 1).astype(f32)
        factor = jnp.where(info[0, :, k : k + 1] == row, info[1, :, k : k + 1], f32(0.0))
        high = factor.astype(bf16)
        low = (factor - high.astype(f32)).astype(bf16)
        for part in (high, low):
            product = jnp.dot(part, value, preferred_element_type=f32)
            total = product if total is None else total + product
    return total


def combine_early(info, order, pieces):
    width = pieces[0].shape[-1]
    tok_rows = info.shape[1]

    def kernel(info_ref, *refs):
        for piece, out in zip(refs, refs[len(pieces) :]):
            out[...] = weighted_sum(info_ref[...], [(k, piece[i]) for i, k in enumerate(order)])

    shapes = [jax.ShapeDtypeStruct((tok_rows, width), f32)] * len(pieces)
    return call(kernel, shapes, [WHOLE] * (1 + len(pieces)))(info, *pieces)


def combine_late(info, early, pieces):
    nodes = len(early)
    order = [k for k, _ in pieces[0]]
    flat = [rows for part in pieces for _, rows in part]
    tok_rows, width = early[0].shape

    def kernel(info_ref, *refs):
        early_refs, late_refs, out_ref = refs[:nodes], refs[nodes:-1], refs[-1]
        node_me = lax.axis_index("node")
        for j in range(nodes):
            mine = [(k, late_refs[j * len(order) + i][...]) for i, k in enumerate(order)]
            value = (early_refs[j][...] + weighted_sum(info_ref[...], mine)).astype(bf16)
            for at in range(nodes):

                @pl.when(node_me ^ j == at)
                def _(value=value, at=at):
                    out_ref[:, at * width : (at + 1) * width] = value

    shapes = [jax.ShapeDtypeStruct((tok_rows, nodes * width), bf16)]
    return call(kernel, shapes, [WHOLE] * (1 + nodes + len(flat)))(info, *early, *flat)[0]


def body(
    tokens,
    routes,
    tenant,
    expert_place,
    router_weight,
    adapter_down,
    adapter_up,
    gate_weight,
    up_weight,
    down_weight,
):
    tok_rows, half_width = tokens.shape
    topk = routes.shape[1]
    eps = lax.axis_size("ep")
    nodes = lax.axis_size("node")
    cap = 5 * tok_rows * topk // (4 * eps)
    out_width = down_weight.shape[3]

    quarter = max(1, eps // 4)
    near = range(1, 2 * quarter)
    middle = range(2 * quarter, 3 * quarter)
    far = range(3 * quarter, eps)
    others = range(1, nodes)
    routes_t = routes.T
    place, *first_out = pack_rows(expert_place, routes_t, tokens, [*middle], cap)
    _, *later_out = pack_rows(expert_place, routes_t, tokens, [0, *near, *far], cap, first_out)
    outgoing = dict(zip([*middle, 0, *near, *far], first_out + later_out))

    blocks = [[outgoing[k]] + [None] * (nodes - 1) for k in range(eps)]
    for k in [*middle, *near]:
        blocks[k][0] = swap(outgoing[k], "ep", k)
    for k in [0, *near]:
        blocks[k][1:] = [swap(outgoing[k], "node", j) for j in others]
    gate_w, up_w, down_w = load(
        [gate_weight[0], up_weight[0], down_weight[0, 0]], [outgoing[0]]
    )
    for k, rows in zip(middle, hold([blocks[k][0] for k in middle], [gate_w, blocks[1][0]])):
        blocks[k] = [rows] + [swap(rows, "node", j) for j in others]
    crossed = [blocks[k][j] for k in near for j in others]
    crossed = hold(crossed + [outgoing[k] for k in far], [blocks[middle[-1]][0]])
    for i, k in enumerate(near):
        for j in others:
            blocks[k][j] = swap(crossed[i * len(others) + j - 1], "ep", k)
    for i, k in enumerate(far):
        blocks[k][0] = swap(crossed[len(near) * len(others) + i], "ep", k)

    def gate_up(chunk, behind):
        rows = [blocks[k][j] for j in range(nodes) for k in chunk]
        own, sent = dots(jnp.concatenate(rows, axis=0), [gate_w, up_w], [f32, bf16], behind)
        return activate(own, lax.all_gather(sent, "sub"))

    def down(chunk, hidden, gather=False, behind=()):
        size = len(chunk) * cap
        by_node = [hidden]
        for i in others:
            sent = regroup(hidden, i, size)
            if gather:
                by_node.append(lax.all_gather(sent, "node"))
            else:
                by_node.append(swap(sent, "node", i))
        out = project(by_node, down_w, behind)
        return out.reshape(nodes, len(chunk), cap, out_width)

    logits = partial_logits(
        tokens, tenant, router_weight, adapter_down, adapter_up, crossed[:1]
    )
    info = route_info(lax.all_gather(logits, "sub"), place, expert_place, routes_t)

    early_chunk, late_chunk = [0, *middle], [*near, *far]
    hidden = gate_up(early_chunk, [info])
    for k in far:
        for j in others:
            blocks[k][j] = swap(blocks[k][0], "node", j)
    early_out = down(early_chunk, hidden, behind=[blocks[k][j] for k in near for j in others])
    hidden = gate_up(late_chunk, [early_out])
    late_out = down(late_chunk, hidden, True)

    back = [early_out[:, 0]]
    back += [swap(early_out[:, i], "ep", k) for i, k in enumerate(early_chunk) if k]
    late = [
        [(k, send(late_out[j, i], k, j)) for i, k in enumerate(late_chunk)] for j in range(nodes)
    ]
    across = [jnp.stack([part[j] for part in back]) for j in range(nodes)]
    across[1:] = hold(across[1:], [late_out])
    across[1:] = [swap(across[j], "node", j) for j in others]
    return combine_late(info, combine_early(info, early_chunk, across), late)


def solution(mesh):
    placed = (
        P(("rep", "ep", "node"), "sub"),
        P(("rep", "ep", "node"), None),
        P(("rep", "ep", "node")),
        P(),
        P("sub", None),
        P("sub", None),
        P(),
        P("ep", "sub", "node"),
        P("ep", "sub", "node"),
        P("ep", "sub", None, "node"),
    )
    return jax.shard_map(
        body, mesh=mesh, in_specs=placed, out_specs=P(("rep", "ep", "node"), "sub"), check_vma=False
    )
```

```python
import functools

import jax
import jax.numpy as jnp
from jax import lax
from jax.experimental import pallas as pl
from jax.experimental.pallas import tpu as pltpu
from jax.sharding import PartitionSpec as P

RANK = 16
ROUTE_SCALE = 2.5
VMEM_LIMIT = 24 * 1024 * 1024
f32 = jnp.float32
bf16 = jnp.bfloat16


def partner(index, step):
    return index ^ step


def swap(value, axis, step):
    count = lax.axis_size(axis)
    return lax.ppermute(value, axis, [(i, partner(i, step)) for i in range(count)])


def send(value, ep_step, node_step):
    if not ep_step and not node_step:
        return value
    if not node_step:
        return swap(value, "ep", ep_step)
    if not ep_step:
        return swap(value, "node", node_step)
    eps, nodes = lax.axis_size("ep"), lax.axis_size("node")
    pairs = [
        (i * nodes + j, partner(i, ep_step) * nodes + partner(j, node_step))
        for i in range(eps)
        for j in range(nodes)
    ]
    return lax.ppermute(value, ("ep", "node"), pairs)


def regroup(rows, step, size):
    count = rows.shape[0] // size
    return jnp.concatenate([rows[(j ^ step) * size : (j ^ step) * size + size] for j in range(count)])


WHOLE = pl.BlockSpec(memory_space=pltpu.VMEM)
ANY = pl.BlockSpec(memory_space=pl.ANY)
IN_HBM = pl.BlockSpec(memory_space=pltpu.HBM)


def call(kernel, out_shape, in_specs, scratch=(), aliases=None):
    return pl.pallas_call(
        kernel,
        out_shape=out_shape,
        in_specs=in_specs,
        out_specs=[ANY if i in (aliases or {}).values() else WHOLE for i in range(len(out_shape))],
        scratch_shapes=list(scratch),
        input_output_aliases=aliases or {},
        compiler_params=pltpu.CompilerParams(vmem_limit_bytes=VMEM_LIMIT),
        cost_estimate=pl.CostEstimate(flops=0, bytes_accessed=0, transcendentals=0),
    )


def in_hbm(value):
    return pltpu.with_memory_space_constraint(value, pltpu.HBM)


def pack_rows(expert_place, routes_t, tokens, order, cap):
    experts = expert_place.shape[0]
    topk, tok_rows = routes_t.shape
    width = tokens.shape[1]

    def kernel(where_hbm, routes_hbm, tokens_hbm, *refs):
        place_ref, *refs = refs
        block_refs, (where_ref, routes_ref, tokens_ref, sems) = refs[: len(order)], refs[len(order) :]
        pairs = [(where_hbm, where_ref), (routes_hbm, routes_ref), (tokens_hbm, tokens_ref)]
        copies = [pltpu.make_async_copy(a, b, sems.at[i]) for i, (a, b) in enumerate(pairs)]
        for copy in copies:
            copy.start()
        copies[0].wait()
        copies[1].wait()
        named_by = routes_ref[...]
        where = where_ref[...] ^ lax.axis_index("ep")
        relative = jnp.zeros_like(named_by)
        for e in range(experts):
            relative = jnp.where(named_by == e, where[:, e : e + 1], relative)
        block = lax.broadcasted_iota(jnp.int32, (experts, tok_rows), 0)
        named = functools.reduce(
            jnp.logical_or, [relative[k : k + 1] == block for k in range(topk)]
        )
        earlier = lax.broadcasted_iota(jnp.int32, (tok_rows, tok_rows), 0) < (
            lax.broadcasted_iota(jnp.int32, (tok_rows, tok_rows), 1)
        )
        before = jnp.dot(
            jnp.where(named, f32(1.0), f32(0.0)).astype(bf16),
            jnp.where(earlier, f32(1.0), f32(0.0)).astype(bf16),
            preferred_element_type=f32,
        )
        place = jnp.where(named, before, f32(-1.0))
        place_ref[...] = place
        row = lax.broadcasted_iota(jnp.int32, (cap, tok_rows), 0).astype(f32)
        copies[2].wait()
        for block_ref, k in zip(block_refs, order):
            placing = jnp.where(place[k : k + 1] == row, f32(1.0), f32(0.0)).astype(bf16)
            block_ref[...] = jnp.dot(
                placing, tokens_ref[...], preferred_element_type=f32
            ).astype(bf16)

    shapes = [jax.ShapeDtypeStruct((experts, tok_rows), f32)]
    shapes += [jax.ShapeDtypeStruct((cap, width), bf16)] * len(order)
    scratch = [
        pltpu.VMEM((1, experts), jnp.int32),
        pltpu.VMEM((topk, tok_rows), jnp.int32),
        pltpu.VMEM((tok_rows, width), bf16),
        pltpu.SemaphoreType.DMA((3,)),
    ]
    return call(kernel, shapes, [IN_HBM] * 3, scratch)(
        in_hbm(expert_place.reshape(1, experts)), in_hbm(routes_t), in_hbm(tokens)
    )


def hold(held, behind):
    count = len(behind)
    shapes = [jax.ShapeDtypeStruct(a.shape, a.dtype) for a in held]
    aliases = {count + i: i for i in range(len(held))}
    specs = [ANY] * (count + len(held))
    return call(lambda *refs: None, shapes, specs, aliases=aliases)(*behind, *held)


def load(arrays, behind):
    count = len(arrays)

    def kernel(*refs):
        fetch(refs[:count], refs[count + len(behind) : -1], refs[-1])

    shapes = [pltpu.VMEM(a.shape, a.dtype) for a in arrays]
    specs = [IN_HBM] * count + [ANY] * len(behind)
    return call(kernel, shapes, specs, [pltpu.SemaphoreType.DMA((count,))])(
        *[in_hbm(a) for a in arrays], *behind
    )


def as_column(row, size):
    same = lax.broadcasted_iota(jnp.int32, (size, size), 0) == (
        lax.broadcasted_iota(jnp.int32, (size, size), 1)
    )
    return jnp.sum(jnp.where(same, row, jnp.zeros_like(row)), axis=1, keepdims=True)


def fetch(sources, places, sems):
    copies = [pltpu.make_async_copy(a, b, sems.at[i]) for i, (a, b) in enumerate(zip(sources, places))]
    for copy in copies:
        copy.start()
    for copy in copies:
        copy.wait()


def partial_logits(tokens, tenant, router_weight, adapter_down, adapter_up, behind):
    tok_rows = tokens.shape[0]
    ranks, experts = adapter_up.shape
    given = [tokens, adapter_down, router_weight.T, adapter_up.T, tenant.reshape(1, tok_rows)]

    def kernel(*refs):
        out_ref, *held, sems = refs[len(given) + len(behind) :]
        fetch(refs[: len(given)], held, sems)
        tokens_ref, down_ref, router_ref, up_ref, tenant_ref = held
        lowrank = jnp.dot(tokens_ref[...], down_ref[...], preferred_element_type=f32)
        owner = (lax.broadcasted_iota(jnp.int32, (tok_rows, ranks), 1) // RANK).astype(f32)
        tenants = as_column(tenant_ref[...].astype(f32), tok_rows)
        lowrank = jnp.where(owner == tenants, lowrank, f32(0.0))
        across = (((1,), (1,)), ((), ()))
        base = lax.dot_general(
            router_ref[...], tokens_ref[...], across, preferred_element_type=f32
        )
        out_ref[...] = base + lax.dot_general(
            up_ref[...].astype(f32),
            lowrank,
            across,
            precision=lax.Precision.HIGHEST,
            preferred_element_type=f32,
        )

    shapes = [jax.ShapeDtypeStruct((experts, tok_rows), f32)]
    specs = [IN_HBM] * len(given) + [ANY] * len(behind)
    scratch = [pltpu.VMEM(a.shape, a.dtype) for a in given]
    scratch.append(pltpu.SemaphoreType.DMA((len(given),)))
    return call(kernel, shapes, specs, scratch)(*[in_hbm(a) for a in given], *behind)[0]


def route_info(parts, place, expert_place, routes_t, behind):
    _, experts, tok_rows = parts.shape
    topk = routes_t.shape[0]
    given = [expert_place.reshape(1, experts), routes_t]

    def kernel(parts_ref, place_ref, where_hbm, routes_hbm, *refs):
        out_ref, where_ref, routes_ref, sems = refs[len(behind) :]
        fetch([where_hbm, routes_hbm], [where_ref, routes_ref], sems)
        score = jax.nn.sigmoid(functools.reduce(jnp.add, [parts_ref[i] for i in range(parts.shape[0])]))
        expert = lax.broadcasted_iota(jnp.int32, (experts, tok_rows), 0)
        chosen = functools.reduce(
            jnp.logical_or, [routes_ref[k : k + 1, :] == expert for k in range(topk)]
        )
        score = jnp.where(chosen, score, f32(0.0))
        weight = ROUTE_SCALE * score / jnp.sum(score, axis=0, keepdims=True)
        slot = where_ref[...] ^ lax.axis_index("ep")
        for r in range(experts):
            here = jnp.zeros((1, tok_rows), f32)
            for e in range(experts):
                here = jnp.where(slot[:, e : e + 1] == r, weight[e : e + 1], here)
            out_ref[0, :, r : r + 1] = as_column(place_ref[r : r + 1, :], tok_rows)
            out_ref[1, :, r : r + 1] = as_column(here, tok_rows)

    shapes = [jax.ShapeDtypeStruct((2, tok_rows, experts), f32)]
    scratch = [pltpu.VMEM(a.shape, a.dtype) for a in given]
    scratch.append(pltpu.SemaphoreType.DMA((len(given),)))
    return call(kernel, shapes, [WHOLE] * 2 + [IN_HBM] * 2 + [ANY] * len(behind), scratch)(
        parts, place, *[in_hbm(a) for a in given], *behind
    )[0]


def activate(own, both):
    count, wide = own.shape

    def kernel(own_ref, both_ref, out_ref):
        total = own_ref[...] + both_ref[1 - lax.axis_index("sub")].astype(f32)
        gate, up = total[:, : wide // 2], total[:, wide // 2 :]
        out_ref[...] = (jax.nn.silu(gate) * up).astype(bf16)

    shapes = [jax.ShapeDtypeStruct((count, wide // 2), bf16)]
    return call(kernel, shapes, [WHOLE] * 2)(own, both)[0]


def dots(rows, weights, kinds, behind):
    count, wide = rows.shape[0], weights[0].shape[1]

    def kernel(rows_ref, *refs):
        for i in range(len(weights)):
            value = jnp.dot(rows_ref[...], refs[i][...], preferred_element_type=f32)
            for out in refs[len(weights) + len(behind) :]:
                out[:, i * wide : (i + 1) * wide] = value.astype(out.dtype)

    shapes = [jax.ShapeDtypeStruct((count, len(weights) * wide), kind) for kind in kinds]
    specs = [WHOLE] * (1 + len(weights)) + [ANY] * len(behind)
    return call(kernel, shapes, specs)(rows, *weights, *behind)


def project(by_node, weight, behind):
    nodes = len(by_node)
    count, part = by_node[0].shape

    def kernel(*refs):
        hidden_refs, weight_ref, out_ref = refs[:nodes], refs[nodes], refs[-1]
        node_me = lax.axis_index("node")
        total = None
        for i in range(nodes):
            node = node_me ^ i
            hidden = hidden_refs[i][...] if by_node[i].ndim == 2 else hidden_refs[i][node]
            at = pl.ds(pl.multiple_of(node * part, part), part)
            value = jnp.dot(hidden, weight_ref[at, :], preferred_element_type=f32)
            total = value if total is None else total + value
        out_ref[...] = total.astype(bf16)

    shapes = [jax.ShapeDtypeStruct((count, weight.shape[1]), bf16)]
    specs = [WHOLE] * (nodes + 1) + [ANY] * len(behind)
    return call(kernel, shapes, specs)(*by_node, weight, *behind)[0]


def weighted_sum(given, pieces):
    return functools.reduce(
        jnp.add, [jnp.dot(given[k], rows, preferred_element_type=f32) for k, rows in pieces]
    )


def combine_early(info, pieces, cap):
    _, tok_rows, count = info.shape
    flat = [rows for part in pieces for _, rows in part]
    width = flat[0].shape[1]

    def kernel(info_ref, *refs):
        given_ref, *sum_refs = refs[len(flat) :]
        row = lax.broadcasted_iota(jnp.int32, (tok_rows, cap), 1).astype(f32)
        low = [None] * count
        for k in range(count):
            hit = info_ref[0, :, k : k + 1] == row
            factor = jnp.where(hit, info_ref[1, :, k : k + 1], f32(0.0))
            given_ref[k] = factor.astype(bf16)
            low[k] = (factor - factor.astype(bf16).astype(f32)).astype(bf16)
        rest = list(refs[: len(flat)])
        for part, out in zip(pieces, sum_refs):
            mine = [(k, rest.pop(0)[...]) for k, _ in part]
            out[...] = weighted_sum(given_ref, mine) + weighted_sum(low, mine)

    shapes = [jax.ShapeDtypeStruct((count, tok_rows, cap), bf16)]
    shapes += [jax.ShapeDtypeStruct((tok_rows, width), f32)] * len(pieces)
    given, *sums = call(kernel, shapes, [WHOLE] * (1 + len(flat)))(info, *flat)
    return given, sums


def combine_late(given, sums, pieces, order, across):
    nodes = len(sums)
    tok_rows, width = sums[0].shape
    flat = [rows for part in pieces for _, rows in part]

    def kernel(given_ref, *refs):
        sum_refs, rest, across_refs = refs[:nodes], list(refs[nodes:-nodes]), refs[-nodes:-1]
        out_ref = refs[-1]
        node_me = lax.axis_index("node")
        for j in range(nodes):
            mine = [(k, rest.pop(0)[...]) for k, _ in pieces[j]]
            if j:
                mine += [(k, across_refs[j - 1][i]) for i, k in enumerate(order)]
            value = (sum_refs[j][...] + weighted_sum(given_ref, mine)).astype(bf16)
            for at in range(nodes):

                @pl.when(node_me ^ j == at)
                def _(value=value, at=at):
                    out_ref[:, at * width : (at + 1) * width] = value

    shapes = [jax.ShapeDtypeStruct((tok_rows, nodes * width), bf16)]
    specs = [WHOLE] * (1 + nodes + len(flat) + len(across))
    return call(kernel, shapes, specs)(given, *sums, *flat, *across)[0]


def body(
    tokens,
    routes,
    tenant,
    expert_place,
    router_weight,
    adapter_down,
    adapter_up,
    gate_weight,
    up_weight,
    down_weight,
):
    tok_rows, half_width = tokens.shape
    topk = routes.shape[1]
    eps = lax.axis_size("ep")
    nodes = lax.axis_size("node")
    cap = 5 * tok_rows * topk // (4 * eps)
    out_width = down_weight.shape[3]

    quarter = max(1, eps // 4)
    near = range(1, 2 * quarter)
    middle = range(2 * quarter, 3 * quarter)
    far = range(3 * quarter, eps)
    others = range(1, nodes)
    routes_t = routes.T
    order = [*middle, 0, *near, *far]
    place, *packed = pack_rows(expert_place, routes_t, tokens, order, cap)
    outgoing = dict(zip(order, packed))

    blocks = [[outgoing[k]] + [None] * (nodes - 1) for k in range(eps)]
    for k in [*middle, *near]:
        blocks[k][0] = swap(outgoing[k], "ep", k)
    for k in [0, *near]:
        blocks[k][1:] = [swap(outgoing[k], "node", j) for j in others]
    gate_w, up_w, down_w = load(
        [gate_weight[0], up_weight[0], down_weight[0, 0]], [outgoing[0]]
    )
    logits = partial_logits(tokens, tenant, router_weight, adapter_down, adapter_up, [gate_w])
    logits = lax.all_gather(logits, "sub")
    for k, rows in zip(far, hold([outgoing[k] for k in far], [logits])):
        blocks[k][0] = swap(rows, "ep", k)
    for k, rows in zip(middle, hold([blocks[k][0] for k in middle], [logits])):
        blocks[k] = [rows] + [swap(rows, "node", j) for j in others]
    crossed = [blocks[k][j] for k in near for j in others]
    crossed = hold(crossed, [blocks[k][0] for k in (middle[-1], *near)])
    for i, k in enumerate(near):
        for j in others:
            blocks[k][j] = swap(crossed[i * len(others) + j - 1], "ep", k)

    def gate_up(chunk, behind):
        rows = [blocks[k][j] for j in range(nodes) for k in chunk]
        own, sent = dots(jnp.concatenate(rows, axis=0), [gate_w, up_w], [f32, bf16], behind)
        return activate(own, lax.all_gather(sent, "sub"))

    def down(chunk, hidden, gather=False, behind=()):
        size = len(chunk) * cap
        by_node = [hidden]
        for i in others:
            sent = regroup(hidden, i, size)
            if gather:
                by_node.append(lax.all_gather(sent, "node"))
            else:
                by_node.append(swap(sent, "node", i))
        out = project(by_node, down_w, behind)
        return out.reshape(nodes, len(chunk), cap, out_width)

    info = route_info(logits, place, expert_place, routes_t, crossed[:1])

    early_chunk, late_chunk = [0, *middle], [*far, *near]
    hidden = gate_up(early_chunk, [info])
    for k, rows in zip(far, hold([blocks[k][0] for k in far], [hidden])):
        blocks[k] = [rows] + [swap(rows, "node", j) for j in others]
    early_out = down(early_chunk, hidden, behind=[blocks[k][j] for k in near for j in others])
    hidden = gate_up(late_chunk, [early_out])
    back = [early_out[:, 0]]
    back += [swap(early_out[:, i], "ep", k) for i, k in enumerate(early_chunk) if k]
    late_out = down(late_chunk, hidden, False, back[1:])
    late = [
        [(k, send(late_out[j, i], k, j)) for i, k in enumerate(late_chunk)] for j in range(nodes)
    ]
    across = hold([jnp.stack([part[j] for part in back]) for j in others], [late_out])
    across = [swap(rows, "node", j) for j, rows in zip(others, across)]
    count = len(far)
    pieces = [part[:count] for part in late]
    pieces[0] = pieces[0] + [(k, part[0]) for k, part in zip(early_chunk, back)]
    given, sums = combine_early(info, pieces, cap)
    return combine_late(given, sums, [part[count:] for part in late], early_chunk, across)


def solution(mesh):
    placed = (
        P(("rep", "ep", "node"), "sub"),
        P(("rep", "ep", "node"), None),
        P(("rep", "ep", "node")),
        P(),
        P("sub", None),
        P("sub", None),
        P(),
        P("ep", "sub", "node"),
        P("ep", "sub", "node"),
        P("ep", "sub", None, "node"),
    )
    return jax.shard_map(
        body, mesh=mesh, in_specs=placed, out_specs=P(("rep", "ep", "node"), "sub"), check_vma=False
    )
```

```python
import functools

import jax
import jax.numpy as jnp
from jax import lax
from jax.experimental import pallas as pl
from jax.experimental.pallas import tpu as pltpu
from jax.sharding import PartitionSpec as P

RANK = 16
ROUTE_SCALE = 2.5
VMEM_LIMIT = 24 * 1024 * 1024
f32 = jnp.float32
bf16 = jnp.bfloat16


def partner(index, step):
    return index ^ step


def swap(value, axis, step):
    count = lax.axis_size(axis)
    return lax.ppermute(value, axis, [(i, partner(i, step)) for i in range(count)])


def send(value, ep_step, node_step):
    if not ep_step and not node_step:
        return value
    if not node_step:
        return swap(value, "ep", ep_step)
    if not ep_step:
        return swap(value, "node", node_step)
    eps, nodes = lax.axis_size("ep"), lax.axis_size("node")
    pairs = [
        (i * nodes + j, partner(i, ep_step) * nodes + partner(j, node_step))
        for i in range(eps)
        for j in range(nodes)
    ]
    return lax.ppermute(value, ("ep", "node"), pairs)


def regroup(rows, step, size):
    count = rows.shape[0] // size
    return jnp.concatenate([rows[(j ^ step) * size : (j ^ step) * size + size] for j in range(count)])


WHOLE = pl.BlockSpec(memory_space=pltpu.VMEM)
ANY = pl.BlockSpec(memory_space=pl.ANY)
IN_HBM = pl.BlockSpec(memory_space=pltpu.HBM)


def call(kernel, out_shape, in_specs, scratch=(), aliases=None):
    return pl.pallas_call(
        kernel,
        out_shape=out_shape,
        in_specs=in_specs,
        out_specs=[ANY if i in (aliases or {}).values() else WHOLE for i in range(len(out_shape))],
        scratch_shapes=list(scratch),
        input_output_aliases=aliases or {},
        compiler_params=pltpu.CompilerParams(vmem_limit_bytes=VMEM_LIMIT),
        cost_estimate=pl.CostEstimate(flops=0, bytes_accessed=0, transcendentals=0),
    )


def in_hbm(value):
    return pltpu.with_memory_space_constraint(value, pltpu.HBM)


def pack_rows(expert_place, routes_t, tokens, order, halved, cap):
    experts = expert_place.shape[0]
    topk, tok_rows = routes_t.shape
    width = tokens.shape[1]

    whole, half = [slice(0, width)], [slice(0, width // 2), slice(width // 2, width)]
    spans = {k: half if k in halved else whole for k in order}

    def kernel(where_hbm, routes_hbm, tokens_hbm, *refs):
        place_ref, *refs = refs
        block_refs, (where_ref, routes_ref, tokens_ref, sems) = list(refs[:-4]), refs[-4:]
        pairs = [(where_hbm, where_ref), (routes_hbm, routes_ref), (tokens_hbm, tokens_ref)]
        copies = [pltpu.make_async_copy(a, b, sems.at[i]) for i, (a, b) in enumerate(pairs)]
        for copy in copies:
            copy.start()
        copies[0].wait()
        copies[1].wait()
        named_by = routes_ref[...]
        where = where_ref[...] ^ lax.axis_index("ep")
        relative = jnp.zeros_like(named_by)
        for e in range(experts):
            relative = jnp.where(named_by == e, where[:, e : e + 1], relative)
        block = lax.broadcasted_iota(jnp.int32, (experts, tok_rows), 0)
        named = functools.reduce(
            jnp.logical_or, [relative[k : k + 1] == block for k in range(topk)]
        )
        earlier = lax.broadcasted_iota(jnp.int32, (tok_rows, tok_rows), 0) < (
            lax.broadcasted_iota(jnp.int32, (tok_rows, tok_rows), 1)
        )
        before = jnp.dot(
            jnp.where(named, f32(1.0), f32(0.0)).astype(bf16),
            jnp.where(earlier, f32(1.0), f32(0.0)).astype(bf16),
            preferred_element_type=f32,
        )
        place = jnp.where(named, before, f32(-1.0))
        place_ref[...] = place
        row = lax.broadcasted_iota(jnp.int32, (cap, tok_rows), 0).astype(f32)
        copies[2].wait()
        for k in order:
            placing = jnp.where(place[k : k + 1] == row, f32(1.0), f32(0.0)).astype(bf16)
            for at in spans[k]:
                block_refs.pop(0)[...] = jnp.dot(
                    placing, tokens_ref[:, at], preferred_element_type=f32
                ).astype(bf16)

    shapes = [jax.ShapeDtypeStruct((experts, tok_rows), f32)]
    shapes += [
        jax.ShapeDtypeStruct((cap, at.stop - at.start), bf16) for k in order for at in spans[k]
    ]
    scratch = [
        pltpu.VMEM((1, experts), jnp.int32),
        pltpu.VMEM((topk, tok_rows), jnp.int32),
        pltpu.VMEM((tok_rows, width), bf16),
        pltpu.SemaphoreType.DMA((3,)),
    ]
    return call(kernel, shapes, [IN_HBM] * 3, scratch)(
        in_hbm(expert_place.reshape(1, experts)), in_hbm(routes_t), in_hbm(tokens)
    )


def hold(held, behind):
    count = len(behind)
    shapes = [jax.ShapeDtypeStruct(a.shape, a.dtype) for a in held]
    aliases = {count + i: i for i in range(len(held))}
    specs = [ANY] * (count + len(held))
    return list(call(lambda *refs: None, shapes, specs, aliases=aliases)(*behind, *held))


def load(arrays, behind):
    count = len(arrays)

    def kernel(*refs):
        fetch(refs[:count], refs[count + len(behind) : -1], refs[-1])

    shapes = [pltpu.VMEM(a.shape, a.dtype) for a in arrays]
    specs = [IN_HBM] * count + [ANY] * len(behind)
    return call(kernel, shapes, specs, [pltpu.SemaphoreType.DMA((count,))])(
        *[in_hbm(a) for a in arrays], *behind
    )


def as_column(row, size):
    same = lax.broadcasted_iota(jnp.int32, (size, size), 0) == (
        lax.broadcasted_iota(jnp.int32, (size, size), 1)
    )
    return jnp.sum(jnp.where(same, row, jnp.zeros_like(row)), axis=1, keepdims=True)


def fetch(sources, places, sems):
    copies = [pltpu.make_async_copy(a, b, sems.at[i]) for i, (a, b) in enumerate(zip(sources, places))]
    for copy in copies:
        copy.start()
    for copy in copies:
        copy.wait()


def partial_logits(tokens, tenant, router_weight, adapter_down, adapter_up, behind):
    tok_rows = tokens.shape[0]
    ranks, experts = adapter_up.shape
    given = [tokens, adapter_down, router_weight.T, adapter_up.T, tenant.reshape(1, tok_rows)]

    def kernel(*refs):
        out_ref, *held, sems = refs[len(given) + len(behind) :]
        fetch(refs[: len(given)], held, sems)
        tokens_ref, down_ref, router_ref, up_ref, tenant_ref = held
        lowrank = jnp.dot(tokens_ref[...], down_ref[...], preferred_element_type=f32)
        owner = (lax.broadcasted_iota(jnp.int32, (tok_rows, ranks), 1) // RANK).astype(f32)
        tenants = as_column(tenant_ref[...].astype(f32), tok_rows)
        lowrank = jnp.where(owner == tenants, lowrank, f32(0.0))
        across = (((1,), (1,)), ((), ()))
        base = lax.dot_general(
            router_ref[...], tokens_ref[...], across, preferred_element_type=f32
        )
        out_ref[...] = base + lax.dot_general(
            up_ref[...].astype(f32),
            lowrank,
            across,
            precision=lax.Precision.HIGHEST,
            preferred_element_type=f32,
        )

    shapes = [jax.ShapeDtypeStruct((experts, tok_rows), f32)]
    specs = [IN_HBM] * len(given) + [ANY] * len(behind)
    scratch = [pltpu.VMEM(a.shape, a.dtype) for a in given]
    scratch.append(pltpu.SemaphoreType.DMA((len(given),)))
    return call(kernel, shapes, specs, scratch)(*[in_hbm(a) for a in given], *behind)[0]


def route_info(parts, place, expert_place, routes_t, behind):
    _, experts, tok_rows = parts.shape
    topk = routes_t.shape[0]
    given = [expert_place.reshape(1, experts), routes_t]

    def kernel(parts_ref, place_ref, where_hbm, routes_hbm, *refs):
        out_ref, where_ref, routes_ref, sems = refs[len(behind) :]
        fetch([where_hbm, routes_hbm], [where_ref, routes_ref], sems)
        score = jax.nn.sigmoid(functools.reduce(jnp.add, [parts_ref[i] for i in range(parts.shape[0])]))
        expert = lax.broadcasted_iota(jnp.int32, (experts, tok_rows), 0)
        chosen = functools.reduce(
            jnp.logical_or, [routes_ref[k : k + 1, :] == expert for k in range(topk)]
        )
        score = jnp.where(chosen, score, f32(0.0))
        weight = ROUTE_SCALE * score / jnp.sum(score, axis=0, keepdims=True)
        slot = where_ref[...] ^ lax.axis_index("ep")
        for r in range(experts):
            here = jnp.zeros((1, tok_rows), f32)
            for e in range(experts):
                here = jnp.where(slot[:, e : e + 1] == r, weight[e : e + 1], here)
            out_ref[0, :, r : r + 1] = as_column(place_ref[r : r + 1, :], tok_rows)
            out_ref[1, :, r : r + 1] = as_column(here, tok_rows)

    shapes = [jax.ShapeDtypeStruct((2, tok_rows, experts), f32)]
    scratch = [pltpu.VMEM(a.shape, a.dtype) for a in given]
    scratch.append(pltpu.SemaphoreType.DMA((len(given),)))
    return call(kernel, shapes, [WHOLE] * 2 + [IN_HBM] * 2 + [ANY] * len(behind), scratch)(
        parts, place, *[in_hbm(a) for a in given], *behind
    )[0]


def activate(own, both):
    count, wide = own.shape

    def kernel(own_ref, both_ref, out_ref):
        total = own_ref[...] + both_ref[1 - lax.axis_index("sub")].astype(f32)
        gate, up = total[:, : wide // 2], total[:, wide // 2 :]
        out_ref[...] = (jax.nn.silu(gate) * up).astype(bf16)

    shapes = [jax.ShapeDtypeStruct((count, wide // 2), bf16)]
    return call(kernel, shapes, [WHOLE] * 2)(own, both)[0]


def dots(rows, weights, kinds, behind):
    count, wide = rows.shape[0], weights[0].shape[1]

    def kernel(rows_ref, *refs):
        for i in range(len(weights)):
            value = jnp.dot(rows_ref[...], refs[i][...], preferred_element_type=f32)
            for out in refs[len(weights) + len(behind) :]:
                out[:, i * wide : (i + 1) * wide] = value.astype(out.dtype)

    shapes = [jax.ShapeDtypeStruct((count, len(weights) * wide), kind) for kind in kinds]
    specs = [WHOLE] * (1 + len(weights)) + [ANY] * len(behind)
    return call(kernel, shapes, specs)(rows, *weights, *behind)


def project(by_node, weight, behind):
    nodes = len(by_node)
    count, part = by_node[0].shape

    def kernel(*refs):
        hidden_refs, weight_ref, out_ref = refs[:nodes], refs[nodes], refs[-1]
        node_me = lax.axis_index("node")
        total = None
        for i in range(nodes):
            node = node_me ^ i
            at = pl.ds(pl.multiple_of(node * part, part), part)
            value = jnp.dot(hidden_refs[i][...], weight_ref[at, :], preferred_element_type=f32)
            total = value if total is None else total + value
        out_ref[...] = total.astype(bf16)

    shapes = [jax.ShapeDtypeStruct((count, weight.shape[1]), bf16)]
    specs = [WHOLE] * (nodes + 1) + [ANY] * len(behind)
    return call(kernel, shapes, specs)(*by_node, weight, *behind)[0]


def weighted_sum(given, pieces):
    return functools.reduce(
        jnp.add, [jnp.dot(given[k], rows, preferred_element_type=f32) for k, rows in pieces]
    )


def combine_early(info, pieces, cap):
    _, tok_rows, count = info.shape
    flat = [rows for part in pieces for _, rows in part]
    width = flat[0].shape[-1]

    def kernel(info_ref, *refs):
        given_ref, *sum_refs = refs[len(flat) :]
        row = lax.broadcasted_iota(jnp.int32, (tok_rows, cap), 1).astype(f32)
        low = [None] * count
        for k in range(count):
            hit = info_ref[0, :, k : k + 1] == row
            factor = jnp.where(hit, info_ref[1, :, k : k + 1], f32(0.0))
            given_ref[k] = factor.astype(bf16)
            low[k] = (factor - factor.astype(bf16).astype(f32)).astype(bf16)
        rest = list(refs[: len(flat)])
        for part, out in zip(pieces, sum_refs):
            mine = []
            for ks, rows in part:
                ref = rest.pop(0)
                mine += [(k, ref[i] if rows.ndim == 3 else ref[...]) for i, k in enumerate(ks)]
            out[...] = weighted_sum(given_ref, mine) + weighted_sum(low, mine)

    shapes = [jax.ShapeDtypeStruct((count, tok_rows, cap), bf16)]
    shapes += [jax.ShapeDtypeStruct((tok_rows, width), f32)] * len(pieces)
    given, *sums = call(kernel, shapes, [WHOLE] * (1 + len(flat)))(info, *flat)
    return given, sums


def combine_late(given, sums, pieces):
    nodes = len(sums)
    tok_rows, width = sums[0].shape
    flat = [rows for part in pieces for _, rows in part]

    def kernel(given_ref, *refs):
        sum_refs, rest, out_ref = refs[:nodes], list(refs[nodes:-1]), refs[-1]
        node_me = lax.axis_index("node")
        for j in range(nodes):
            mine = [(k, rest.pop(0)[...]) for k, _ in pieces[j]]
            value = (sum_refs[j][...] + weighted_sum(given_ref, mine)).astype(bf16)
            for at in range(nodes):

                @pl.when(node_me ^ j == at)
                def _(value=value, at=at):
                    out_ref[:, at * width : (at + 1) * width] = value

    shapes = [jax.ShapeDtypeStruct((tok_rows, nodes * width), bf16)]
    return call(kernel, shapes, [WHOLE] * (1 + nodes + len(flat)))(given, *sums, *flat)[0]


def body(
    tokens,
    routes,
    tenant,
    expert_place,
    router_weight,
    adapter_down,
    adapter_up,
    gate_weight,
    up_weight,
    down_weight,
):
    tok_rows, half_width = tokens.shape
    topk = routes.shape[1]
    eps = lax.axis_size("ep")
    nodes = lax.axis_size("node")
    cap = 5 * tok_rows * topk // (4 * eps)
    out_width = down_weight.shape[3]

    quarter = max(1, eps // 4)
    near = range(1, 2 * quarter)
    middle = range(2 * quarter, 3 * quarter)
    far = range(3 * quarter, eps)
    others = range(1, nodes)
    routes_t = routes.T
    order = [*middle, 0, *near, *far]
    place, *packed = pack_rows(expert_place, routes_t, tokens, order, middle, cap)
    outgoing = {k: [packed.pop(0) for _ in range(2 if k in middle else 1)] for k in order}

    blocks = [[outgoing[k]] + [None] * (nodes - 1) for k in range(eps)]
    for k in [*middle, *near]:
        blocks[k][0] = [swap(part, "ep", k) for part in outgoing[k]]
    for k in [0, *near]:
        blocks[k][1:] = [[swap(outgoing[k][0], "node", j)] for j in others]
    gate_w, up_w, down_w = load(
        [gate_weight[0], up_weight[0], down_weight[0, 0]], [outgoing[0][0]]
    )
    firsts = hold([blocks[k][0][0] for k in middle], [gate_w])
    logits = partial_logits(tokens, tenant, router_weight, adapter_down, adapter_up, firsts[:1])
    logits = lax.all_gather(logits, "sub")
    for k, part in zip(middle, firsts):
        blocks[k][0][0] = part
        blocks[k][1:] = [[swap(part, "node", j)] for j in others]
    seconds = hold(
        [blocks[k][0][1] for k in middle], [logits] + [blocks[0][j][0] for j in others]
    )
    for k, part in zip(middle, seconds):
        blocks[k][0][1] = part
        for j in others:
            blocks[k][j].append(swap(part, "node", j))
    for k, rows in zip(far, hold([outgoing[k][0] for k in far], [logits])):
        blocks[k][0] = [swap(rows, "ep", k)]
    crossed = [blocks[k][j][0] for k in near for j in others]
    crossed = hold(crossed, seconds[:1] + [blocks[k][0][0] for k in near])
    anchor = crossed[:1]
    for k in near:
        blocks[k][1:] = [[swap(crossed.pop(0), "ep", k)] for j in others]

    def gate_up(chunk, behind):
        rows = [jnp.concatenate(blocks[k][j], axis=1) for j in range(nodes) for k in chunk]
        own, sent = dots(jnp.concatenate(rows, axis=0), [gate_w, up_w], [f32, bf16], behind)
        return activate(own, lax.all_gather(sent, "sub"))

    def down(chunk, hidden, behind=()):
        size = len(chunk) * cap
        by_node = [hidden]
        for i in others:
            by_node.append(swap(regroup(hidden, i, size), "node", i))
        out = project(by_node, down_w, behind)
        return out.reshape(nodes, len(chunk), cap, out_width)

    info = route_info(logits, place, expert_place, routes_t, anchor)

    early_chunk, late_chunk = [0, *middle], [*far, *near]
    hidden = gate_up(early_chunk, [info])
    for k, rows in zip(far, hold([blocks[k][0][0] for k in far], [hidden])):
        blocks[k] = [[rows]] + [[swap(rows, "node", j)] for j in others]
    early_out = down(early_chunk, hidden)
    hidden = gate_up(late_chunk, [early_out])
    back = [early_out[:, 0]]
    back += [swap(early_out[:, i], "ep", k) for i, k in enumerate(early_chunk) if k]
    late_out = down(late_chunk, hidden, back[1:])
    late = [
        [(k, send(late_out[j, i], k, j)) for i, k in enumerate(late_chunk)] for j in range(nodes)
    ]
    across = [jnp.stack([part[j] for part in back]) for j in others]
    across = [swap(rows, "node", j) for j, rows in zip(others, across)]
    count = len(far)
    pieces = [[([k], rows) for k, rows in part[:count]] for part in late]
    pieces[0] += [([k], part[0]) for k, part in zip(early_chunk, back)]
    for part, rows in zip(pieces[1:], across):
        part.append((early_chunk, rows))
    given, sums = combine_early(info, pieces, cap)
    return combine_late(given, sums, [part[count:] for part in late])


def solution(mesh):
    placed = (
        P(("rep", "ep", "node"), "sub"),
        P(("rep", "ep", "node"), None),
        P(("rep", "ep", "node")),
        P(),
        P("sub", None),
        P("sub", None),
        P(),
        P("ep", "sub", "node"),
        P("ep", "sub", "node"),
        P("ep", "sub", None, "node"),
    )
    return jax.shard_map(
        body, mesh=mesh, in_specs=placed, out_specs=P(("rep", "ep", "node"), "sub"), check_vma=False
    )
```

```python
import functools

import jax
import jax.numpy as jnp
from jax import lax
from jax.experimental import pallas as pl
from jax.experimental.pallas import tpu as pltpu
from jax.sharding import PartitionSpec as P

RANK = 16
ROUTE_SCALE = 2.5
VMEM_LIMIT = 24 * 1024 * 1024
f32 = jnp.float32
bf16 = jnp.bfloat16


def partner(index, step):
    return index ^ step


def swap(value, axis, step):
    count = lax.axis_size(axis)
    return lax.ppermute(value, axis, [(i, partner(i, step)) for i in range(count)])


def send(value, ep_step, node_step):
    if not ep_step and not node_step:
        return value
    if not node_step:
        return swap(value, "ep", ep_step)
    if not ep_step:
        return swap(value, "node", node_step)
    eps, nodes = lax.axis_size("ep"), lax.axis_size("node")
    pairs = [
        (i * nodes + j, partner(i, ep_step) * nodes + partner(j, node_step))
        for i in range(eps)
        for j in range(nodes)
    ]
    return lax.ppermute(value, ("ep", "node"), pairs)


def regroup(rows, step, size):
    count = rows.shape[0] // size
    return jnp.concatenate([rows[(j ^ step) * size : (j ^ step) * size + size] for j in range(count)])


WHOLE = pl.BlockSpec(memory_space=pltpu.VMEM)
ANY = pl.BlockSpec(memory_space=pl.ANY)
IN_HBM = pl.BlockSpec(memory_space=pltpu.HBM)


def call(kernel, out_shape, in_specs, scratch=(), aliases=None):
    return pl.pallas_call(
        kernel,
        out_shape=out_shape,
        in_specs=in_specs,
        out_specs=[ANY if i in (aliases or {}).values() else WHOLE for i in range(len(out_shape))],
        scratch_shapes=list(scratch),
        input_output_aliases=aliases or {},
        compiler_params=pltpu.CompilerParams(vmem_limit_bytes=VMEM_LIMIT),
        cost_estimate=pl.CostEstimate(flops=0, bytes_accessed=0, transcendentals=0),
    )


def in_hbm(value):
    return pltpu.with_memory_space_constraint(value, pltpu.HBM)


def pack_rows(expert_place, routes_t, tokens, order, halved, cap):
    experts = expert_place.shape[0]
    topk, tok_rows = routes_t.shape
    width = tokens.shape[1]

    whole, half = [slice(0, width)], [slice(0, width // 2), slice(width // 2, width)]
    spans = {k: half if k in halved else whole for k in order}

    def kernel(where_hbm, routes_hbm, tokens_hbm, *refs):
        place_ref, *refs = refs
        block_refs, (where_ref, routes_ref, tokens_ref, sems) = list(refs[:-4]), refs[-4:]
        pairs = [(where_hbm, where_ref), (routes_hbm, routes_ref), (tokens_hbm, tokens_ref)]
        copies = [pltpu.make_async_copy(a, b, sems.at[i]) for i, (a, b) in enumerate(pairs)]
        for copy in copies:
            copy.start()
        copies[0].wait()
        copies[1].wait()
        named_by = routes_ref[...]
        where = where_ref[...] ^ lax.axis_index("ep")
        relative = jnp.zeros_like(named_by)
        for e in range(experts):
            relative = jnp.where(named_by == e, where[:, e : e + 1], relative)
        block = lax.broadcasted_iota(jnp.int32, (experts, tok_rows), 0)
        named = functools.reduce(
            jnp.logical_or, [relative[k : k + 1] == block for k in range(topk)]
        )
        earlier = lax.broadcasted_iota(jnp.int32, (tok_rows, tok_rows), 0) < (
            lax.broadcasted_iota(jnp.int32, (tok_rows, tok_rows), 1)
        )
        before = jnp.dot(
            jnp.where(named, f32(1.0), f32(0.0)).astype(bf16),
            jnp.where(earlier, f32(1.0), f32(0.0)).astype(bf16),
            preferred_element_type=f32,
        )
        place = jnp.where(named, before, f32(-1.0))
        place_ref[...] = place
        row = lax.broadcasted_iota(jnp.int32, (cap, tok_rows), 0).astype(f32)
        copies[2].wait()
        for k in order:
            placing = jnp.where(place[k : k + 1] == row, f32(1.0), f32(0.0)).astype(bf16)
            for at in spans[k]:
                block_refs.pop(0)[...] = jnp.dot(
                    placing, tokens_ref[:, at], preferred_element_type=f32
                ).astype(bf16)

    shapes = [jax.ShapeDtypeStruct((experts, tok_rows), f32)]
    shapes += [
        jax.ShapeDtypeStruct((cap, at.stop - at.start), bf16) for k in order for at in spans[k]
    ]
    scratch = [
        pltpu.VMEM((1, experts), jnp.int32),
        pltpu.VMEM((topk, tok_rows), jnp.int32),
        pltpu.VMEM((tok_rows, width), bf16),
        pltpu.SemaphoreType.DMA((3,)),
    ]
    return call(kernel, shapes, [IN_HBM] * 3, scratch)(
        in_hbm(expert_place.reshape(1, experts)), in_hbm(routes_t), in_hbm(tokens)
    )


def hold(held, behind):
    count = len(behind)
    shapes = [jax.ShapeDtypeStruct(a.shape, a.dtype) for a in held]
    aliases = {count + i: i for i in range(len(held))}
    specs = [ANY] * (count + len(held))
    return list(call(lambda *refs: None, shapes, specs, aliases=aliases)(*behind, *held))


def as_column(row, size):
    same = lax.broadcasted_iota(jnp.int32, (size, size), 0) == (
        lax.broadcasted_iota(jnp.int32, (size, size), 1)
    )
    return jnp.sum(jnp.where(same, row, jnp.zeros_like(row)), axis=1, keepdims=True)


def fetch(sources, places, sems):
    copies = [pltpu.make_async_copy(a, b, sems.at[i]) for i, (a, b) in enumerate(zip(sources, places))]
    for copy in copies:
        copy.start()
    for copy in copies:
        copy.wait()


def load_and_route(arrays, tokens, tenant, router_weight, adapter_down, adapter_up, behind):
    count = len(arrays)
    tok_rows = tokens.shape[0]
    ranks, experts = adapter_up.shape
    given = [tokens, adapter_down, router_weight.T, adapter_up.T, tenant.reshape(1, tok_rows)]
    total = count + len(given)

    def kernel(*refs):
        taken, rest = refs[total + len(behind) :][:count], refs[total + len(behind) + count :]
        out_ref, *held, sems = rest
        pairs = list(zip(refs[count:total], held)) + list(zip(refs[:count], taken))
        copies = [pltpu.make_async_copy(a, b, sems.at[i]) for i, (a, b) in enumerate(pairs)]
        for copy in copies:
            copy.start()
        for copy in copies[: len(given)]:
            copy.wait()
        tokens_ref, down_ref, router_ref, up_ref, tenant_ref = held
        lowrank = jnp.dot(tokens_ref[...], down_ref[...], preferred_element_type=f32)
        owner = (lax.broadcasted_iota(jnp.int32, (tok_rows, ranks), 1) // RANK).astype(f32)
        tenants = as_column(tenant_ref[...].astype(f32), tok_rows)
        lowrank = jnp.where(owner == tenants, lowrank, f32(0.0))
        across = (((1,), (1,)), ((), ()))
        base = lax.dot_general(
            router_ref[...], tokens_ref[...], across, preferred_element_type=f32
        )
        out_ref[...] = base + lax.dot_general(
            up_ref[...].astype(f32),
            lowrank,
            across,
            precision=lax.Precision.HIGHEST,
            preferred_element_type=f32,
        )
        for copy in copies[len(given) :]:
            copy.wait()

    shapes = [pltpu.VMEM(a.shape, a.dtype) for a in arrays]
    shapes.append(jax.ShapeDtypeStruct((experts, tok_rows), f32))
    specs = [IN_HBM] * total + [ANY] * len(behind)
    scratch = [pltpu.VMEM(a.shape, a.dtype) for a in given]
    scratch.append(pltpu.SemaphoreType.DMA((total,)))
    *taken, logits = call(kernel, shapes, specs, scratch)(
        *[in_hbm(a) for a in (*arrays, *given)], *behind
    )
    return taken, logits


def route_info(parts, place, expert_place, routes_t, behind):
    _, experts, tok_rows = parts.shape
    topk = routes_t.shape[0]
    given = [expert_place.reshape(1, experts), routes_t]

    def kernel(parts_ref, place_ref, where_hbm, routes_hbm, *refs):
        out_ref, where_ref, routes_ref, sems = refs[len(behind) :]
        fetch([where_hbm, routes_hbm], [where_ref, routes_ref], sems)
        score = jax.nn.sigmoid(functools.reduce(jnp.add, [parts_ref[i] for i in range(parts.shape[0])]))
        expert = lax.broadcasted_iota(jnp.int32, (experts, tok_rows), 0)
        chosen = functools.reduce(
            jnp.logical_or, [routes_ref[k : k + 1, :] == expert for k in range(topk)]
        )
        score = jnp.where(chosen, score, f32(0.0))
        weight = ROUTE_SCALE * score / jnp.sum(score, axis=0, keepdims=True)
        slot = where_ref[...] ^ lax.axis_index("ep")
        for r in range(experts):
            here = jnp.zeros((1, tok_rows), f32)
            for e in range(experts):
                here = jnp.where(slot[:, e : e + 1] == r, weight[e : e + 1], here)
            out_ref[0, :, r : r + 1] = as_column(place_ref[r : r + 1, :], tok_rows)
            out_ref[1, :, r : r + 1] = as_column(here, tok_rows)

    shapes = [jax.ShapeDtypeStruct((2, tok_rows, experts), f32)]
    scratch = [pltpu.VMEM(a.shape, a.dtype) for a in given]
    scratch.append(pltpu.SemaphoreType.DMA((len(given),)))
    return call(kernel, shapes, [WHOLE] * 2 + [IN_HBM] * 2 + [ANY] * len(behind), scratch)(
        parts, place, *[in_hbm(a) for a in given], *behind
    )[0]


def activate(own, both):
    count, wide = own.shape

    def kernel(own_ref, both_ref, out_ref):
        total = own_ref[...] + both_ref[1 - lax.axis_index("sub")].astype(f32)
        gate, up = total[:, : wide // 2], total[:, wide // 2 :]
        out_ref[...] = (jax.nn.silu(gate) * up).astype(bf16)

    shapes = [jax.ShapeDtypeStruct((count, wide // 2), bf16)]
    return call(kernel, shapes, [WHOLE] * 2)(own, both)[0]


def dots(rows, weights, kinds, behind):
    count, wide = rows.shape[0], weights[0].shape[1]

    def kernel(rows_ref, *refs):
        for i in range(len(weights)):
            value = jnp.dot(rows_ref[...], refs[i][...], preferred_element_type=f32)
            for out in refs[len(weights) + len(behind) :]:
                out[:, i * wide : (i + 1) * wide] = value.astype(out.dtype)

    shapes = [jax.ShapeDtypeStruct((count, len(weights) * wide), kind) for kind in kinds]
    specs = [WHOLE] * (1 + len(weights)) + [ANY] * len(behind)
    return call(kernel, shapes, specs)(rows, *weights, *behind)


def project(by_node, weight, behind):
    nodes = len(by_node)
    count, part = by_node[0].shape

    def kernel(*refs):
        hidden_refs, weight_ref, out_ref = refs[:nodes], refs[nodes], refs[-1]
        node_me = lax.axis_index("node")
        total = None
        for i in range(nodes):
            node = node_me ^ i
            at = pl.ds(pl.multiple_of(node * part, part), part)
            value = jnp.dot(hidden_refs[i][...], weight_ref[at, :], preferred_element_type=f32)
            total = value if total is None else total + value
        out_ref[...] = total.astype(bf16)

    shapes = [jax.ShapeDtypeStruct((count, weight.shape[1]), bf16)]
    specs = [WHOLE] * (nodes + 1) + [ANY] * len(behind)
    return call(kernel, shapes, specs)(*by_node, weight, *behind)[0]


def weighted_sum(given, pieces):
    return functools.reduce(
        jnp.add, [jnp.dot(given[k], rows, preferred_element_type=f32) for k, rows in pieces]
    )


def combine_early(info, pieces, cap):
    _, tok_rows, count = info.shape
    flat = [rows for part in pieces for _, rows in part]
    width = flat[0].shape[-1]

    def kernel(info_ref, *refs):
        given_ref, *sum_refs = refs[len(flat) :]
        row = lax.broadcasted_iota(jnp.int32, (tok_rows, cap), 1).astype(f32)
        low = [None] * count
        for k in range(count):
            hit = info_ref[0, :, k : k + 1] == row
            factor = jnp.where(hit, info_ref[1, :, k : k + 1], f32(0.0))
            given_ref[k] = factor.astype(bf16)
            low[k] = (factor - factor.astype(bf16).astype(f32)).astype(bf16)
        rest = list(refs[: len(flat)])
        for part, out in zip(pieces, sum_refs):
            mine = []
            for ks, rows in part:
                ref = rest.pop(0)
                mine += [(k, ref[i] if rows.ndim == 3 else ref[...]) for i, k in enumerate(ks)]
            out[...] = weighted_sum(given_ref, mine) + weighted_sum(low, mine)

    shapes = [jax.ShapeDtypeStruct((count, tok_rows, cap), bf16)]
    shapes += [jax.ShapeDtypeStruct((tok_rows, width), f32)] * len(pieces)
    given, *sums = call(kernel, shapes, [WHOLE] * (1 + len(flat)))(info, *flat)
    return given, sums


def combine_late(given, sums, pieces):
    nodes = len(sums)
    tok_rows, width = sums[0].shape
    flat = [rows for part in pieces for _, rows in part]

    def kernel(given_ref, *refs):
        sum_refs, rest, out_ref = refs[:nodes], list(refs[nodes:-1]), refs[-1]
        node_me = lax.axis_index("node")
        for j in range(nodes):
            mine = [(k, rest.pop(0)[...]) for k, _ in pieces[j]]
            value = (sum_refs[j][...] + weighted_sum(given_ref, mine)).astype(bf16)
            for at in range(nodes):

                @pl.when(node_me ^ j == at)
                def _(value=value, at=at):
                    out_ref[:, at * width : (at + 1) * width] = value

    shapes = [jax.ShapeDtypeStruct((tok_rows, nodes * width), bf16)]
    return call(kernel, shapes, [WHOLE] * (1 + nodes + len(flat)))(given, *sums, *flat)[0]


def body(
    tokens,
    routes,
    tenant,
    expert_place,
    router_weight,
    adapter_down,
    adapter_up,
    gate_weight,
    up_weight,
    down_weight,
):
    tok_rows, half_width = tokens.shape
    topk = routes.shape[1]
    eps = lax.axis_size("ep")
    nodes = lax.axis_size("node")
    cap = 5 * tok_rows * topk // (4 * eps)
    out_width = down_weight.shape[3]

    quarter = max(1, eps // 4)
    near = range(1, 2 * quarter)
    middle = range(2 * quarter, 3 * quarter)
    far = range(3 * quarter, eps)
    others = range(1, nodes)
    routes_t = routes.T
    order = [*middle, 0, *near, *far]
    place, *packed = pack_rows(expert_place, routes_t, tokens, order, middle, cap)
    outgoing = {k: [packed.pop(0) for _ in range(2 if k in middle else 1)] for k in order}

    blocks = [[outgoing[k]] + [None] * (nodes - 1) for k in range(eps)]
    for k in [*middle, *near]:
        blocks[k][0] = [swap(part, "ep", k) for part in outgoing[k]]
    for k in [0, *near]:
        blocks[k][1:] = [[swap(outgoing[k][0], "node", j)] for j in others]
    (gate_w, up_w, down_w), logits = load_and_route(
        [gate_weight[0], up_weight[0], down_weight[0, 0]],
        tokens,
        tenant,
        router_weight,
        adapter_down,
        adapter_up,
        outgoing[0],
    )
    firsts = hold([blocks[k][0][0] for k in middle], [logits])
    logits = lax.all_gather(hold([logits], firsts[:1])[0], "sub")
    for k, part in zip(middle, firsts):
        blocks[k][0][0] = part
        blocks[k][1:] = [[swap(part, "node", j)] for j in others]
    seconds = hold(
        [blocks[k][0][1] for k in middle], [logits] + [blocks[0][j][0] for j in others]
    )
    for k, part in zip(middle, seconds):
        blocks[k][0][1] = part
        for j in others:
            blocks[k][j].append(swap(part, "node", j))
    for k, rows in zip(far, hold([outgoing[k][0] for k in far], [logits])):
        blocks[k][0] = [swap(rows, "ep", k)]
    crossed = [blocks[k][j][0] for k in near for j in others]
    crossed = hold(crossed, seconds[:1] + [blocks[k][0][0] for k in near])
    anchor = crossed[:1]
    for k in near:
        blocks[k][1:] = [[swap(crossed.pop(0), "ep", k)] for j in others]

    def gate_up(chunk, behind):
        rows = [jnp.concatenate(blocks[k][j], axis=1) for j in range(nodes) for k in chunk]
        own, sent = dots(jnp.concatenate(rows, axis=0), [gate_w, up_w], [f32, bf16], behind)
        return activate(own, lax.all_gather(sent, "sub"))

    def down(chunk, hidden, behind=()):
        size = len(chunk) * cap
        by_node = [hidden]
        for i in others:
            by_node.append(swap(regroup(hidden, i, size), "node", i))
        out = project(by_node, down_w, behind)
        return out.reshape(nodes, len(chunk), cap, out_width)

    info = route_info(logits, place, expert_place, routes_t, anchor)

    early_chunk, late_chunk = [0, *middle], [*far, *near]
    hidden = gate_up(early_chunk, [info])
    for k, rows in zip(far, hold([blocks[k][0][0] for k in far], [hidden])):
        blocks[k] = [[rows]] + [[swap(rows, "node", j)] for j in others]
    early_out = down(early_chunk, hidden)
    hidden = gate_up(late_chunk, [early_out])
    back = [early_out[:, 0]]
    back += [swap(early_out[:, i], "ep", k) for i, k in enumerate(early_chunk) if k]
    late_out = down(late_chunk, hidden, back[1:])
    late = [
        [(k, send(late_out[j, i], k, j)) for i, k in enumerate(late_chunk)] for j in range(nodes)
    ]
    across = [jnp.stack([part[j] for part in back]) for j in others]
    across = [swap(rows, "node", j) for j, rows in zip(others, across)]
    count = len(far)
    pieces = [[([k], rows) for k, rows in part[:count]] for part in late]
    pieces[0] += [([k], part[0]) for k, part in zip(early_chunk, back)]
    for part, rows in zip(pieces[1:], across):
        part.append((early_chunk, rows))
    given, sums = combine_early(info, pieces, cap)
    return combine_late(given, sums, [part[count:] for part in late])


def solution(mesh):
    placed = (
        P(("rep", "ep", "node"), "sub"),
        P(("rep", "ep", "node"), None),
        P(("rep", "ep", "node")),
        P(),
        P("sub", None),
        P("sub", None),
        P(),
        P("ep", "sub", "node"),
        P("ep", "sub", "node"),
        P("ep", "sub", None, "node"),
    )
    return jax.shard_map(
        body, mesh=mesh, in_specs=placed, out_specs=P(("rep", "ep", "node"), "sub"), check_vma=False
    )
```

```python
import functools

import jax
import jax.numpy as jnp
from jax import lax
from jax.experimental import pallas as pl
from jax.experimental.pallas import tpu as pltpu
from jax.sharding import PartitionSpec as P

RANK = 16
ROUTE_SCALE = 2.5
VMEM_LIMIT = 24 * 1024 * 1024
f32 = jnp.float32
bf16 = jnp.bfloat16


def partner(index, step):
    return index ^ step


def swap(value, axis, step):
    count = lax.axis_size(axis)
    return lax.ppermute(value, axis, [(i, partner(i, step)) for i in range(count)])


def send(value, ep_step, node_step):
    if not ep_step and not node_step:
        return value
    if not node_step:
        return swap(value, "ep", ep_step)
    if not ep_step:
        return swap(value, "node", node_step)
    eps, nodes = lax.axis_size("ep"), lax.axis_size("node")
    pairs = [
        (i * nodes + j, partner(i, ep_step) * nodes + partner(j, node_step))
        for i in range(eps)
        for j in range(nodes)
    ]
    return lax.ppermute(value, ("ep", "node"), pairs)


def regroup(rows, step, size):
    count = rows.shape[0] // size
    return jnp.concatenate([rows[(j ^ step) * size : (j ^ step) * size + size] for j in range(count)])


WHOLE = pl.BlockSpec(memory_space=pltpu.VMEM)
ANY = pl.BlockSpec(memory_space=pl.ANY)
IN_HBM = pl.BlockSpec(memory_space=pltpu.HBM)


def call(kernel, out_shape, in_specs, scratch=(), aliases=None):
    return pl.pallas_call(
        kernel,
        out_shape=out_shape,
        in_specs=in_specs,
        out_specs=[ANY if i in (aliases or {}).values() else WHOLE for i in range(len(out_shape))],
        scratch_shapes=list(scratch),
        input_output_aliases=aliases or {},
        compiler_params=pltpu.CompilerParams(vmem_limit_bytes=VMEM_LIMIT),
        cost_estimate=pl.CostEstimate(flops=0, bytes_accessed=0, transcendentals=0),
    )


def in_hbm(value):
    return pltpu.with_memory_space_constraint(value, pltpu.HBM)


def pack_rows(expert_place, routes_t, tokens, order, halved, cap):
    experts = expert_place.shape[0]
    topk, tok_rows = routes_t.shape
    width = tokens.shape[1]

    whole, half = [slice(0, width)], [slice(0, width // 2), slice(width // 2, width)]
    spans = {k: half if k in halved else whole for k in order}

    def kernel(where_hbm, routes_hbm, tokens_hbm, *refs):
        place_ref, *refs = refs
        block_refs, (where_ref, routes_ref, tokens_ref, sems) = list(refs[:-4]), refs[-4:]
        pairs = [(where_hbm, where_ref), (routes_hbm, routes_ref), (tokens_hbm, tokens_ref)]
        copies = [pltpu.make_async_copy(a, b, sems.at[i]) for i, (a, b) in enumerate(pairs)]
        for copy in copies:
            copy.start()
        copies[0].wait()
        copies[1].wait()
        named_by = routes_ref[...]
        where = where_ref[...] ^ lax.axis_index("ep")
        relative = jnp.zeros_like(named_by)
        for e in range(experts):
            relative = jnp.where(named_by == e, where[:, e : e + 1], relative)
        block = lax.broadcasted_iota(jnp.int32, (experts, tok_rows), 0)
        named = functools.reduce(
            jnp.logical_or, [relative[k : k + 1] == block for k in range(topk)]
        )
        earlier = lax.broadcasted_iota(jnp.int32, (tok_rows, tok_rows), 0) < (
            lax.broadcasted_iota(jnp.int32, (tok_rows, tok_rows), 1)
        )
        before = jnp.dot(
            jnp.where(named, f32(1.0), f32(0.0)).astype(bf16),
            jnp.where(earlier, f32(1.0), f32(0.0)).astype(bf16),
            preferred_element_type=f32,
        )
        place = jnp.where(named, before, f32(-1.0))
        place_ref[...] = place
        row = lax.broadcasted_iota(jnp.int32, (cap, tok_rows), 0).astype(f32)
        copies[2].wait()
        for k in order:
            placing = jnp.where(place[k : k + 1] == row, f32(1.0), f32(0.0)).astype(bf16)
            for at in spans[k]:
                block_refs.pop(0)[...] = jnp.dot(
                    placing, tokens_ref[:, at], preferred_element_type=f32
                ).astype(bf16)

    shapes = [jax.ShapeDtypeStruct((experts, tok_rows), f32)]
    shapes += [
        jax.ShapeDtypeStruct((cap, at.stop - at.start), bf16) for k in order for at in spans[k]
    ]
    scratch = [
        pltpu.VMEM((1, experts), jnp.int32),
        pltpu.VMEM((topk, tok_rows), jnp.int32),
        pltpu.VMEM((tok_rows, width), bf16),
        pltpu.SemaphoreType.DMA((3,)),
    ]
    return call(kernel, shapes, [IN_HBM] * 3, scratch)(
        in_hbm(expert_place.reshape(1, experts)), in_hbm(routes_t), in_hbm(tokens)
    )


def hold(held, behind):
    count = len(behind)
    shapes = [jax.ShapeDtypeStruct(a.shape, a.dtype) for a in held]
    aliases = {count + i: i for i in range(len(held))}
    specs = [ANY] * (count + len(held))
    return list(call(lambda *refs: None, shapes, specs, aliases=aliases)(*behind, *held))


def as_column(row, size):
    same = lax.broadcasted_iota(jnp.int32, (size, size), 0) == (
        lax.broadcasted_iota(jnp.int32, (size, size), 1)
    )
    return jnp.sum(jnp.where(same, row, jnp.zeros_like(row)), axis=1, keepdims=True)


def fetch(sources, places, sems):
    copies = [pltpu.make_async_copy(a, b, sems.at[i]) for i, (a, b) in enumerate(zip(sources, places))]
    for copy in copies:
        copy.start()
    for copy in copies:
        copy.wait()


def load_and_route(arrays, tokens, tenant, router_weight, adapter_down, adapter_up, behind):
    count = len(arrays)
    tok_rows = tokens.shape[0]
    ranks, experts = adapter_up.shape
    given = [tokens, adapter_down, router_weight.T, adapter_up.T, tenant.reshape(1, tok_rows)]
    total = count + len(given)

    def kernel(*refs):
        taken, rest = refs[total + len(behind) :][:count], refs[total + len(behind) + count :]
        out_ref, *held, sems = rest
        pairs = list(zip(refs[count:total], held)) + list(zip(refs[:count], taken))
        copies = [pltpu.make_async_copy(a, b, sems.at[i]) for i, (a, b) in enumerate(pairs)]
        for copy in copies:
            copy.start()
        for copy in copies[: len(given)]:
            copy.wait()
        tokens_ref, down_ref, router_ref, up_ref, tenant_ref = held
        lowrank = jnp.dot(tokens_ref[...], down_ref[...], preferred_element_type=f32)
        owner = (lax.broadcasted_iota(jnp.int32, (tok_rows, ranks), 1) // RANK).astype(f32)
        tenants = as_column(tenant_ref[...].astype(f32), tok_rows)
        lowrank = jnp.where(owner == tenants, lowrank, f32(0.0))
        across = (((1,), (1,)), ((), ()))
        base = lax.dot_general(
            router_ref[...], tokens_ref[...], across, preferred_element_type=f32
        )
        out_ref[...] = base + lax.dot_general(
            up_ref[...].astype(f32),
            lowrank,
            across,
            precision=lax.Precision.HIGHEST,
            preferred_element_type=f32,
        )
        for copy in copies[len(given) :]:
            copy.wait()

    shapes = [pltpu.VMEM(a.shape, a.dtype) for a in arrays]
    shapes.append(jax.ShapeDtypeStruct((experts, tok_rows), f32))
    specs = [IN_HBM] * total + [ANY] * len(behind)
    scratch = [pltpu.VMEM(a.shape, a.dtype) for a in given]
    scratch.append(pltpu.SemaphoreType.DMA((total,)))
    *taken, logits = call(kernel, shapes, specs, scratch)(
        *[in_hbm(a) for a in (*arrays, *given)], *behind
    )
    return taken, logits


def route_info(parts, place, expert_place, routes_t, behind):
    _, experts, tok_rows = parts.shape
    topk = routes_t.shape[0]
    given = [expert_place.reshape(1, experts), routes_t]

    def kernel(parts_ref, place_ref, where_hbm, routes_hbm, *refs):
        out_ref, where_ref, routes_ref, sems = refs[len(behind) :]
        fetch([where_hbm, routes_hbm], [where_ref, routes_ref], sems)
        score = jax.nn.sigmoid(functools.reduce(jnp.add, [parts_ref[i] for i in range(parts.shape[0])]))
        expert = lax.broadcasted_iota(jnp.int32, (experts, tok_rows), 0)
        chosen = functools.reduce(
            jnp.logical_or, [routes_ref[k : k + 1, :] == expert for k in range(topk)]
        )
        score = jnp.where(chosen, score, f32(0.0))
        weight = ROUTE_SCALE * score / jnp.sum(score, axis=0, keepdims=True)
        slot = where_ref[...] ^ lax.axis_index("ep")
        for r in range(experts):
            here = jnp.zeros((1, tok_rows), f32)
            for e in range(experts):
                here = jnp.where(slot[:, e : e + 1] == r, weight[e : e + 1], here)
            out_ref[0, :, r : r + 1] = as_column(place_ref[r : r + 1, :], tok_rows)
            out_ref[1, :, r : r + 1] = as_column(here, tok_rows)

    shapes = [jax.ShapeDtypeStruct((2, tok_rows, experts), f32)]
    scratch = [pltpu.VMEM(a.shape, a.dtype) for a in given]
    scratch.append(pltpu.SemaphoreType.DMA((len(given),)))
    return call(kernel, shapes, [WHOLE] * 2 + [IN_HBM] * 2 + [ANY] * len(behind), scratch)(
        parts, place, *[in_hbm(a) for a in given], *behind
    )[0]


def activate(own, both):
    count, wide = own.shape

    def kernel(own_ref, both_ref, out_ref):
        total = own_ref[...] + both_ref[1 - lax.axis_index("sub")].astype(f32)
        gate, up = total[:, : wide // 2], total[:, wide // 2 :]
        out_ref[...] = (jax.nn.silu(gate) * up).astype(bf16)

    shapes = [jax.ShapeDtypeStruct((count, wide // 2), bf16)]
    return call(kernel, shapes, [WHOLE] * 2)(own, both)[0]


def dots(rows, weights, kinds, behind):
    count, wide = rows.shape[0], weights[0].shape[1]

    def kernel(rows_ref, *refs):
        for i in range(len(weights)):
            value = jnp.dot(rows_ref[...], refs[i][...], preferred_element_type=f32)
            for out in refs[len(weights) + len(behind) :]:
                out[:, i * wide : (i + 1) * wide] = value.astype(out.dtype)

    shapes = [jax.ShapeDtypeStruct((count, len(weights) * wide), kind) for kind in kinds]
    specs = [WHOLE] * (1 + len(weights)) + [ANY] * len(behind)
    return call(kernel, shapes, specs)(rows, *weights, *behind)


def project(by_node, weight, behind):
    nodes = len(by_node)
    count, part = by_node[0].shape

    def kernel(*refs):
        hidden_refs, weight_ref, out_ref = refs[:nodes], refs[nodes], refs[-1]
        node_me = lax.axis_index("node")
        total = None
        for i in range(nodes):
            node = node_me ^ i
            at = pl.ds(pl.multiple_of(node * part, part), part)
            value = jnp.dot(hidden_refs[i][...], weight_ref[at, :], preferred_element_type=f32)
            total = value if total is None else total + value
        out_ref[...] = total.astype(bf16)

    shapes = [jax.ShapeDtypeStruct((count, weight.shape[1]), bf16)]
    specs = [WHOLE] * (nodes + 1) + [ANY] * len(behind)
    return call(kernel, shapes, specs)(*by_node, weight, *behind)[0]


def weighted_sum(given, pieces):
    return functools.reduce(
        jnp.add, [jnp.dot(given[k], rows, preferred_element_type=f32) for k, rows in pieces]
    )


def combine_early(info, pieces, cap):
    _, tok_rows, count = info.shape
    flat = [rows for part in pieces for _, rows in part]
    width = flat[0].shape[-1]

    def kernel(info_ref, *refs):
        given_ref, *sum_refs = refs[len(flat) :]
        row = lax.broadcasted_iota(jnp.int32, (tok_rows, cap), 1).astype(f32)
        low = [None] * count
        for k in range(count):
            hit = info_ref[0, :, k : k + 1] == row
            factor = jnp.where(hit, info_ref[1, :, k : k + 1], f32(0.0))
            given_ref[k] = factor.astype(bf16)
            low[k] = (factor - factor.astype(bf16).astype(f32)).astype(bf16)
        rest = list(refs[: len(flat)])
        for part, out in zip(pieces, sum_refs):
            mine = []
            for ks, rows in part:
                ref = rest.pop(0)
                mine += [(k, ref[i] if rows.ndim == 3 else ref[...]) for i, k in enumerate(ks)]
            out[...] = weighted_sum(given_ref, mine) + weighted_sum(low, mine)

    shapes = [jax.ShapeDtypeStruct((count, tok_rows, cap), bf16)]
    shapes += [jax.ShapeDtypeStruct((tok_rows, width), f32)] * len(pieces)
    given, *sums = call(kernel, shapes, [WHOLE] * (1 + len(flat)))(info, *flat)
    return given, sums


def combine_late(given, sums, pieces):
    nodes = len(sums)
    tok_rows, width = sums[0].shape
    flat = [rows for part in pieces for _, rows in part]

    def kernel(given_ref, *refs):
        sum_refs, rest, out_ref = refs[:nodes], list(refs[nodes:-1]), refs[-1]
        node_me = lax.axis_index("node")
        for j in range(nodes):
            mine = [(k, rest.pop(0)[...]) for k, _ in pieces[j]]
            value = sum_refs[j][...]
            if mine:
                value = value + weighted_sum(given_ref, mine)
            value = value.astype(bf16)
            for at in range(nodes):

                @pl.when(node_me ^ j == at)
                def _(value=value, at=at):
                    out_ref[:, at * width : (at + 1) * width] = value

    shapes = [jax.ShapeDtypeStruct((tok_rows, nodes * width), bf16)]
    return call(kernel, shapes, [WHOLE] * (1 + nodes + len(flat)))(given, *sums, *flat)[0]


def body(
    tokens,
    routes,
    tenant,
    expert_place,
    router_weight,
    adapter_down,
    adapter_up,
    gate_weight,
    up_weight,
    down_weight,
):
    tok_rows, half_width = tokens.shape
    topk = routes.shape[1]
    eps = lax.axis_size("ep")
    nodes = lax.axis_size("node")
    cap = 5 * tok_rows * topk // (4 * eps)
    out_width = down_weight.shape[3]

    quarter = max(1, eps // 4)
    near = range(1, 2 * quarter)
    middle = range(2 * quarter, 3 * quarter)
    far = range(3 * quarter, eps)
    others = range(1, nodes)
    routes_t = routes.T
    order = [*middle, 0, *near, *far]
    place, *packed = pack_rows(expert_place, routes_t, tokens, order, middle, cap)
    outgoing = {k: [packed.pop(0) for _ in range(2 if k in middle else 1)] for k in order}

    blocks = [[outgoing[k]] + [None] * (nodes - 1) for k in range(eps)]
    for k in [*middle, *near]:
        blocks[k][0] = [swap(part, "ep", k) for part in outgoing[k]]
    for k in [0, *near]:
        blocks[k][1:] = [[swap(outgoing[k][0], "node", j)] for j in others]
    (gate_w, up_w, down_w), logits = load_and_route(
        [gate_weight[0], up_weight[0], down_weight[0, 0]],
        tokens,
        tenant,
        router_weight,
        adapter_down,
        adapter_up,
        outgoing[0],
    )
    firsts = hold([blocks[k][0][0] for k in middle], [logits])
    logits = lax.all_gather(hold([logits], firsts[:1])[0], "sub")
    for k, part in zip(middle, firsts):
        blocks[k][0][0] = part
        blocks[k][1:] = [[swap(part, "node", j)] for j in others]
    seconds = hold(
        [blocks[k][0][1] for k in middle], [logits] + [blocks[0][j][0] for j in others]
    )
    for k, part in zip(middle, seconds):
        blocks[k][0][1] = part
        for j in others:
            blocks[k][j].append(swap(part, "node", j))
    for k, rows in zip(far, hold([outgoing[k][0] for k in far], [logits])):
        blocks[k][0] = [swap(rows, "ep", k)]
    crossed = [blocks[k][j][0] for k in near for j in others]
    crossed = hold(crossed, seconds[:1] + [blocks[k][0][0] for k in near])
    anchor = crossed[:1]
    for k in near:
        blocks[k][1:] = [[swap(crossed.pop(0), "ep", k)] for j in others]

    def gate_up(chunk, behind):
        rows = [jnp.concatenate(blocks[k][j], axis=1) for j in range(nodes) for k in chunk]
        own, sent = dots(jnp.concatenate(rows, axis=0), [gate_w, up_w], [f32, bf16], behind)
        return activate(own, lax.all_gather(sent, "sub"))

    def down(chunk, hidden, behind=()):
        size = len(chunk) * cap
        by_node = [hidden]
        for i in others:
            by_node.append(swap(regroup(hidden, i, size), "node", i))
        out = project(by_node, down_w, behind)
        return out.reshape(nodes, len(chunk), cap, out_width)

    info = route_info(logits, place, expert_place, routes_t, anchor)

    early_chunk, late_chunk = [0, *middle], [*far, *near]
    hidden = gate_up(early_chunk, [info])
    for k, rows in zip(far, hold([blocks[k][0][0] for k in far], [hidden])):
        blocks[k] = [[rows]] + [[swap(rows, "node", j)] for j in others]
    early_out = down(early_chunk, hidden)
    hidden = gate_up(late_chunk, [early_out])
    back = [early_out[:, 0]]
    back += [swap(early_out[:, i], "ep", k) for i, k in enumerate(early_chunk) if k]
    late_out = down(late_chunk, hidden, back[1:])
    late = [
        [(k, send(late_out[j, i], k, j)) for i, k in enumerate(late_chunk)] for j in range(nodes)
    ]
    across = [jnp.stack([part[j] for part in back]) for j in others]
    across = [swap(rows, "node", j) for j, rows in zip(others, across)]
    count = len(far)
    pieces = [[([k], rows) for k, rows in part[:count]] for part in late]
    pieces[0] += [([k], part[0]) for k, part in zip(early_chunk, back)]
    pieces[0] += [([k], rows) for k, rows in late[0][count:]]
    for part, rows in zip(pieces[1:], across):
        part.append((early_chunk, rows))
    given, sums = combine_early(info, pieces, cap)
    return combine_late(given, sums, [[]] + [part[count:] for part in late[1:]])


def solution(mesh):
    placed = (
        P(("rep", "ep", "node"), "sub"),
        P(("rep", "ep", "node"), None),
        P(("rep", "ep", "node")),
        P(),
        P("sub", None),
        P("sub", None),
        P(),
        P("ep", "sub", "node"),
        P("ep", "sub", "node"),
        P("ep", "sub", None, "node"),
    )
    return jax.shard_map(
        body, mesh=mesh, in_specs=placed, out_specs=P(("rep", "ep", "node"), "sub"), check_vma=False
    )
```

```python
import functools

import jax
import jax.numpy as jnp
from jax import lax
from jax.experimental import pallas as pl
from jax.experimental.pallas import tpu as pltpu
from jax.sharding import PartitionSpec as P

RANK = 16
ROUTE_SCALE = 2.5
VMEM_LIMIT = 24 * 1024 * 1024
f32 = jnp.float32
bf16 = jnp.bfloat16


def partner(index, step):
    return index ^ step


def swap(value, axis, step):
    count = lax.axis_size(axis)
    return lax.ppermute(value, axis, [(i, partner(i, step)) for i in range(count)])


def send(value, ep_step, node_step):
    if not ep_step and not node_step:
        return value
    if not node_step:
        return swap(value, "ep", ep_step)
    if not ep_step:
        return swap(value, "node", node_step)
    eps, nodes = lax.axis_size("ep"), lax.axis_size("node")
    pairs = [
        (i * nodes + j, partner(i, ep_step) * nodes + partner(j, node_step))
        for i in range(eps)
        for j in range(nodes)
    ]
    return lax.ppermute(value, ("ep", "node"), pairs)


def regroup(rows, step, size):
    count = rows.shape[0] // size
    return jnp.concatenate([rows[(j ^ step) * size : (j ^ step) * size + size] for j in range(count)])


WHOLE = pl.BlockSpec(memory_space=pltpu.VMEM)
ANY = pl.BlockSpec(memory_space=pl.ANY)
IN_HBM = pl.BlockSpec(memory_space=pltpu.HBM)


def call(kernel, out_shape, in_specs, scratch=(), aliases=None):
    return pl.pallas_call(
        kernel,
        out_shape=out_shape,
        in_specs=in_specs,
        out_specs=[ANY if i in (aliases or {}).values() else WHOLE for i in range(len(out_shape))],
        scratch_shapes=list(scratch),
        input_output_aliases=aliases or {},
        compiler_params=pltpu.CompilerParams(vmem_limit_bytes=VMEM_LIMIT),
        cost_estimate=pl.CostEstimate(flops=0, bytes_accessed=0, transcendentals=0),
    )


def in_hbm(value):
    return pltpu.with_memory_space_constraint(value, pltpu.HBM)


def pack_rows(expert_place, routes_t, tokens, order, halved, cap):
    experts = expert_place.shape[0]
    topk, tok_rows = routes_t.shape
    width = tokens.shape[1]

    whole, half = [slice(0, width)], [slice(0, width // 2), slice(width // 2, width)]
    spans = {k: half if k in halved else whole for k in order}

    def kernel(where_hbm, routes_hbm, tokens_hbm, *refs):
        place_ref, *refs = refs
        block_refs, (where_ref, routes_ref, tokens_ref, sems) = list(refs[:-4]), refs[-4:]
        pairs = [(where_hbm, where_ref), (routes_hbm, routes_ref), (tokens_hbm, tokens_ref)]
        copies = [pltpu.make_async_copy(a, b, sems.at[i]) for i, (a, b) in enumerate(pairs)]
        for copy in copies:
            copy.start()
        copies[0].wait()
        copies[1].wait()
        named_by = routes_ref[...]
        where = where_ref[...] ^ lax.axis_index("ep")
        relative = jnp.zeros_like(named_by)
        for e in range(experts):
            relative = jnp.where(named_by == e, where[:, e : e + 1], relative)
        block = lax.broadcasted_iota(jnp.int32, (experts, tok_rows), 0)
        named = functools.reduce(
            jnp.logical_or, [relative[k : k + 1] == block for k in range(topk)]
        )
        earlier = lax.broadcasted_iota(jnp.int32, (tok_rows, tok_rows), 0) < (
            lax.broadcasted_iota(jnp.int32, (tok_rows, tok_rows), 1)
        )
        before = jnp.dot(
            jnp.where(named, f32(1.0), f32(0.0)).astype(bf16),
            jnp.where(earlier, f32(1.0), f32(0.0)).astype(bf16),
            preferred_element_type=f32,
        )
        place = jnp.where(named, before, f32(-1.0))
        place_ref[...] = place
        row = lax.broadcasted_iota(jnp.int32, (cap, tok_rows), 0).astype(f32)
        copies[2].wait()
        for k in order:
            placing = jnp.where(place[k : k + 1] == row, f32(1.0), f32(0.0)).astype(bf16)
            for at in spans[k]:
                block_refs.pop(0)[...] = jnp.dot(
                    placing, tokens_ref[:, at], preferred_element_type=f32
                ).astype(bf16)

    shapes = [jax.ShapeDtypeStruct((experts, tok_rows), f32)]
    shapes += [
        jax.ShapeDtypeStruct((cap, at.stop - at.start), bf16) for k in order for at in spans[k]
    ]
    scratch = [
        pltpu.VMEM((1, experts), jnp.int32),
        pltpu.VMEM((topk, tok_rows), jnp.int32),
        pltpu.VMEM((tok_rows, width), bf16),
        pltpu.SemaphoreType.DMA((3,)),
    ]
    return call(kernel, shapes, [IN_HBM] * 3, scratch)(
        in_hbm(expert_place.reshape(1, experts)), in_hbm(routes_t), in_hbm(tokens)
    )


def hold(held, behind):
    count = len(behind)
    shapes = [jax.ShapeDtypeStruct(a.shape, a.dtype) for a in held]
    aliases = {count + i: i for i in range(len(held))}
    specs = [ANY] * (count + len(held))
    return list(call(lambda *refs: None, shapes, specs, aliases=aliases)(*behind, *held))


def as_column(row, size):
    same = lax.broadcasted_iota(jnp.int32, (size, size), 0) == (
        lax.broadcasted_iota(jnp.int32, (size, size), 1)
    )
    return jnp.sum(jnp.where(same, row, jnp.zeros_like(row)), axis=1, keepdims=True)


def fetch(sources, places, sems):
    copies = [pltpu.make_async_copy(a, b, sems.at[i]) for i, (a, b) in enumerate(zip(sources, places))]
    for copy in copies:
        copy.start()
    for copy in copies:
        copy.wait()


def load_and_route(arrays, tokens, tenant, router_weight, adapter_down, adapter_up, behind):
    count = len(arrays)
    tok_rows = tokens.shape[0]
    ranks, experts = adapter_up.shape
    given = [tokens, adapter_down, router_weight.T, adapter_up.T, tenant.reshape(1, tok_rows)]
    total = count + len(given)

    def kernel(*refs):
        taken, rest = refs[total + len(behind) :][:count], refs[total + len(behind) + count :]
        out_ref, *held, sems = rest
        pairs = list(zip(refs[count:total], held)) + list(zip(refs[:count], taken))
        copies = [pltpu.make_async_copy(a, b, sems.at[i]) for i, (a, b) in enumerate(pairs)]
        for copy in copies:
            copy.start()
        for copy in copies[: len(given)]:
            copy.wait()
        tokens_ref, down_ref, router_ref, up_ref, tenant_ref = held
        lowrank = jnp.dot(tokens_ref[...], down_ref[...], preferred_element_type=f32)
        owner = (lax.broadcasted_iota(jnp.int32, (tok_rows, ranks), 1) // RANK).astype(f32)
        tenants = as_column(tenant_ref[...].astype(f32), tok_rows)
        lowrank = jnp.where(owner == tenants, lowrank, f32(0.0))
        across = (((1,), (1,)), ((), ()))
        base = lax.dot_general(
            router_ref[...], tokens_ref[...], across, preferred_element_type=f32
        )
        out_ref[...] = base + lax.dot_general(
            up_ref[...].astype(f32),
            lowrank,
            across,
            precision=lax.Precision.HIGHEST,
            preferred_element_type=f32,
        )
        for copy in copies[len(given) :]:
            copy.wait()

    shapes = [pltpu.VMEM(a.shape, a.dtype) for a in arrays]
    shapes.append(jax.ShapeDtypeStruct((experts, tok_rows), f32))
    specs = [IN_HBM] * total + [ANY] * len(behind)
    scratch = [pltpu.VMEM(a.shape, a.dtype) for a in given]
    scratch.append(pltpu.SemaphoreType.DMA((total,)))
    *taken, logits = call(kernel, shapes, specs, scratch)(
        *[in_hbm(a) for a in (*arrays, *given)], *behind
    )
    return taken, logits


def route_info(parts, place, expert_place, routes_t, behind):
    _, experts, tok_rows = parts.shape
    topk = routes_t.shape[0]
    given = [expert_place.reshape(1, experts), routes_t]

    def kernel(parts_ref, place_ref, where_hbm, routes_hbm, *refs):
        out_ref, where_ref, routes_ref, sems = refs[len(behind) :]
        fetch([where_hbm, routes_hbm], [where_ref, routes_ref], sems)
        score = jax.nn.sigmoid(functools.reduce(jnp.add, [parts_ref[i] for i in range(parts.shape[0])]))
        expert = lax.broadcasted_iota(jnp.int32, (experts, tok_rows), 0)
        chosen = functools.reduce(
            jnp.logical_or, [routes_ref[k : k + 1, :] == expert for k in range(topk)]
        )
        score = jnp.where(chosen, score, f32(0.0))
        weight = ROUTE_SCALE * score / jnp.sum(score, axis=0, keepdims=True)
        slot = where_ref[...] ^ lax.axis_index("ep")
        for r in range(experts):
            here = jnp.zeros((1, tok_rows), f32)
            for e in range(experts):
                here = jnp.where(slot[:, e : e + 1] == r, weight[e : e + 1], here)
            out_ref[0, :, r : r + 1] = as_column(place_ref[r : r + 1, :], tok_rows)
            out_ref[1, :, r : r + 1] = as_column(here, tok_rows)

    shapes = [jax.ShapeDtypeStruct((2, tok_rows, experts), f32)]
    scratch = [pltpu.VMEM(a.shape, a.dtype) for a in given]
    scratch.append(pltpu.SemaphoreType.DMA((len(given),)))
    return call(kernel, shapes, [WHOLE] * 2 + [IN_HBM] * 2 + [ANY] * len(behind), scratch)(
        parts, place, *[in_hbm(a) for a in given], *behind
    )[0]


def activate(own, both):
    count, wide = own.shape

    def kernel(own_ref, both_ref, out_ref):
        total = own_ref[...] + both_ref[1 - lax.axis_index("sub")].astype(f32)
        gate, up = total[:, : wide // 2], total[:, wide // 2 :]
        out_ref[...] = (jax.nn.silu(gate) * up).astype(bf16)

    shapes = [jax.ShapeDtypeStruct((count, wide // 2), bf16)]
    return call(kernel, shapes, [WHOLE] * 2)(own, both)[0]


def dots(rows, weights, kinds, behind):
    count, wide = rows.shape[0], weights[0].shape[1]

    def kernel(rows_ref, *refs):
        for i in range(len(weights)):
            value = jnp.dot(rows_ref[...], refs[i][...], preferred_element_type=f32)
            for out in refs[len(weights) + len(behind) :]:
                out[:, i * wide : (i + 1) * wide] = value.astype(out.dtype)

    shapes = [jax.ShapeDtypeStruct((count, len(weights) * wide), kind) for kind in kinds]
    specs = [WHOLE] * (1 + len(weights)) + [ANY] * len(behind)
    return call(kernel, shapes, specs)(rows, *weights, *behind)


def project(by_node, weight, behind):
    nodes = len(by_node)
    count, part = by_node[0].shape

    def kernel(*refs):
        hidden_refs, weight_ref, out_ref = refs[:nodes], refs[nodes], refs[-1]
        node_me = lax.axis_index("node")
        total = None
        for i in range(nodes):
            node = node_me ^ i
            at = pl.ds(pl.multiple_of(node * part, part), part)
            value = jnp.dot(hidden_refs[i][...], weight_ref[at, :], preferred_element_type=f32)
            total = value if total is None else total + value
        out_ref[...] = total.astype(bf16)

    shapes = [jax.ShapeDtypeStruct((count, weight.shape[1]), bf16)]
    specs = [WHOLE] * (nodes + 1) + [ANY] * len(behind)
    return call(kernel, shapes, specs)(*by_node, weight, *behind)[0]


def weighted_sum(given, pieces):
    return functools.reduce(
        jnp.add, [jnp.dot(given[k], rows, preferred_element_type=f32) for k, rows in pieces]
    )


def combine_early(info, pieces, cap):
    _, tok_rows, count = info.shape
    flat = [rows for part in pieces for _, rows in part]
    width = flat[0].shape[-1]

    def kernel(info_ref, *refs):
        given_ref, *sum_refs = refs[len(flat) :]
        row = lax.broadcasted_iota(jnp.int32, (tok_rows, cap), 1).astype(f32)
        low = [None] * count
        for k in range(count):
            hit = info_ref[0, :, k : k + 1] == row
            factor = jnp.where(hit, info_ref[1, :, k : k + 1], f32(0.0))
            given_ref[k] = factor.astype(bf16)
            low[k] = (factor - factor.astype(bf16).astype(f32)).astype(bf16)
        rest = list(refs[: len(flat)])
        for part, out in zip(pieces, sum_refs):
            mine = []
            for ks, rows in part:
                ref = rest.pop(0)
                mine += [(k, ref[i] if rows.ndim == 3 else ref[...]) for i, k in enumerate(ks)]
            out[...] = weighted_sum(given_ref, mine)

    shapes = [jax.ShapeDtypeStruct((count, tok_rows, cap), bf16)]
    shapes += [jax.ShapeDtypeStruct((tok_rows, width), f32)] * len(pieces)
    given, *sums = call(kernel, shapes, [WHOLE] * (1 + len(flat)))(info, *flat)
    return given, sums


def combine_late(given, sums, pieces):
    nodes = len(sums)
    tok_rows, width = sums[0].shape
    flat = [rows for part in pieces for _, rows in part]

    def kernel(given_ref, *refs):
        sum_refs, rest, out_ref = refs[:nodes], list(refs[nodes:-1]), refs[-1]
        node_me = lax.axis_index("node")
        for j in range(nodes):
            mine = [(k, rest.pop(0)[...]) for k, _ in pieces[j]]
            value = sum_refs[j][...]
            if mine:
                value = value + weighted_sum(given_ref, mine)
            value = value.astype(bf16)
            for at in range(nodes):

                @pl.when(node_me ^ j == at)
                def _(value=value, at=at):
                    out_ref[:, at * width : (at + 1) * width] = value

    shapes = [jax.ShapeDtypeStruct((tok_rows, nodes * width), bf16)]
    return call(kernel, shapes, [WHOLE] * (1 + nodes + len(flat)))(given, *sums, *flat)[0]


def body(
    tokens,
    routes,
    tenant,
    expert_place,
    router_weight,
    adapter_down,
    adapter_up,
    gate_weight,
    up_weight,
    down_weight,
):
    tok_rows, half_width = tokens.shape
    topk = routes.shape[1]
    eps = lax.axis_size("ep")
    nodes = lax.axis_size("node")
    cap = 5 * tok_rows * topk // (4 * eps)
    out_width = down_weight.shape[3]

    quarter = max(1, eps // 4)
    near = range(1, 2 * quarter)
    middle = range(2 * quarter, 3 * quarter)
    far = range(3 * quarter, eps)
    others = range(1, nodes)
    routes_t = routes.T
    order = [*middle, 0, *near, *far]
    place, *packed = pack_rows(expert_place, routes_t, tokens, order, middle, cap)
    outgoing = {k: [packed.pop(0) for _ in range(2 if k in middle else 1)] for k in order}

    blocks = [[outgoing[k]] + [None] * (nodes - 1) for k in range(eps)]
    for k in [*middle, *near]:
        blocks[k][0] = [swap(part, "ep", k) for part in outgoing[k]]
    for k in [0, *near]:
        blocks[k][1:] = [[swap(outgoing[k][0], "node", j)] for j in others]
    (gate_w, up_w, down_w), logits = load_and_route(
        [gate_weight[0], up_weight[0], down_weight[0, 0]],
        tokens,
        tenant,
        router_weight,
        adapter_down,
        adapter_up,
        outgoing[0],
    )
    firsts = hold([blocks[k][0][0] for k in middle], [logits])
    logits = lax.all_gather(hold([logits], firsts[:1])[0], "sub")
    for k, part in zip(middle, firsts):
        blocks[k][0][0] = part
        blocks[k][1:] = [[swap(part, "node", j)] for j in others]
    seconds = hold(
        [blocks[k][0][1] for k in middle], [logits] + [blocks[0][j][0] for j in others]
    )
    for k, part in zip(middle, seconds):
        blocks[k][0][1] = part
        for j in others:
            blocks[k][j].append(swap(part, "node", j))
    for k, rows in zip(far, hold([outgoing[k][0] for k in far], [logits])):
        blocks[k][0] = [swap(rows, "ep", k)]
    crossed = [blocks[k][j][0] for k in near for j in others]
    crossed = hold(crossed, seconds[:1] + [blocks[k][0][0] for k in near])
    anchor = crossed[:1]
    for k in near:
        blocks[k][1:] = [[swap(crossed.pop(0), "ep", k)] for j in others]

    def gate_up(chunk, behind):
        rows = [jnp.concatenate(blocks[k][j], axis=1) for j in range(nodes) for k in chunk]
        own, sent = dots(jnp.concatenate(rows, axis=0), [gate_w, up_w], [f32, bf16], behind)
        return activate(own, lax.all_gather(sent, "sub"))

    def down(chunk, hidden, behind=()):
        size = len(chunk) * cap
        by_node = [hidden]
        for i in others:
            by_node.append(swap(regroup(hidden, i, size), "node", i))
        out = project(by_node, down_w, behind)
        return out.reshape(nodes, len(chunk), cap, out_width)

    info = route_info(logits, place, expert_place, routes_t, anchor)

    early_chunk, late_chunk = [0, *middle], [*far, *near]
    hidden = gate_up(early_chunk, [info])
    for k, rows in zip(far, hold([blocks[k][0][0] for k in far], [hidden])):
        blocks[k] = [[rows]] + [[swap(rows, "node", j)] for j in others]
    early_out = down(early_chunk, hidden)
    hidden = gate_up(late_chunk, [early_out])
    back = [early_out[:, 0]]
    back += [swap(early_out[:, i], "ep", k) for i, k in enumerate(early_chunk) if k]
    late_out = down(late_chunk, hidden, back[1:])
    late = [
        [(k, send(late_out[j, i], k, j)) for i, k in enumerate(late_chunk)] for j in range(nodes)
    ]
    across = [jnp.stack([part[j] for part in back]) for j in others]
    across = [swap(rows, "node", j) for j, rows in zip(others, across)]
    count = len(far)
    pieces = [[([k], rows) for k, rows in part[:count]] for part in late]
    pieces[0] += [([k], part[0]) for k, part in zip(early_chunk, back)]
    pieces[0] += [([k], rows) for k, rows in late[0][count:]]
    for part, rows in zip(pieces[1:], across):
        part.append((early_chunk, rows))
    given, sums = combine_early(info, pieces, cap)
    return combine_late(given, sums, [[]] + [part[count:] for part in late[1:]])


def solution(mesh):
    placed = (
        P(("rep", "ep", "node"), "sub"),
        P(("rep", "ep", "node"), None),
        P(("rep", "ep", "node")),
        P(),
        P("sub", None),
        P("sub", None),
        P(),
        P("ep", "sub", "node"),
        P("ep", "sub", "node"),
        P("ep", "sub", None, "node"),
    )
    return jax.shard_map(
        body, mesh=mesh, in_specs=placed, out_specs=P(("rep", "ep", "node"), "sub"), check_vma=False
    )
```
